256 devices in a mesh: grp: 8 (over z_lo, y), rep: 32 (over x, z_hi, core).
Axes of the slice: x: 4, y: 4, z: 8 (z_hi: 4, z_lo: 2; z = z_hi * 2 + z_lo), core: 2. Of those that a mesh axis runs over, the one named last changes fastest.
Arguments:
- tokens: bfloat16 [1024, 14848], P('grp', 'rep'), may hold values from -6 to 6
- first_weight: bfloat16 [14848, 7424], P('rep', 'grp'), may hold values from -0.046875 to 0.046875
- second_weight: bfloat16 [7424, 14848], P('grp', 'rep'), may hold values from -0.0625 to 0.0625
- cotangent: bfloat16 [1024, 14848], P('grp', 'rep'), may hold values from -6 to 6
Outputs:
- output: bfloat16 [1024, 14848], P('grp', 'rep')
- input_grad: bfloat16 [1024, 14848], P('grp', 'rep')
- first_grad: bfloat16 [14848, 7424], P('rep', 'grp')
- second_grad: bfloat16 [7424, 14848], P('grp', 'rep')
The draws below stay inside these ranges and needn't reach their ends.
All inputs are finite; a program needn't handle non-finite values.
Results may differ from the reference program's by a relative error of at most 0.017.
Values may be sent and summed in bfloat16 or wider, within the bound.
No kernel may reach another device: no remote copies, remote signals or barrier semaphores. Data moves between devices by JAX's collectives and lax.ppermute only.
A program may use at most 128 MiB of HBM per device.

```python
import math
import jax
import jax.numpy as jnp
from jax import lax

D = 14848
F = 7424
TOK_G = 128
TOKENS = 1024
N_GRP = 8


def block_levels(rng, shape, shards, least, top_value):
    factor_of, own = 1.0, jax.random.fold_in(rng, 6)
    for axis_at, shards_of in shards:
        heights = jnp.exp(jax.random.uniform(jax.random.fold_in(own, axis_at), (shards_of,), jnp.float32, least / len(shards), top_value / len(shards)))
        factor_of = factor_of * jnp.repeat(heights, shape[axis_at] // shards_of).reshape([-1 if axis == axis_at else 1 for axis in range(len(shape))])
    return factor_of


def noise(stream_key, extent, scale, most, pieces=(), held_as=jnp.bfloat16):
    drawn = jax.random.normal(stream_key, extent, jnp.float32) * scale
    if len(pieces) > 0:
        drawn = block_levels(stream_key, extent, pieces, -0.22, 0.18) * drawn
    return jnp.clip(drawn, min=-most, max=most).astype(held_as)


def setup_inputs(seed: int = 0) -> dict:
    streams_of = jax.random.split(jax.random.key(seed), 5)
    return {
        "tokens": noise(streams_of[0], (TOKENS, D), 1.0, 6.0, ((0, 8), (1, 32))),
        "first_weight": noise(streams_of[1], (D, F), D ** -0.5, 0.046875, ((0, 32), (1, 8))),
        "second_weight": noise(streams_of[2], (F, D), F ** -0.5, 0.0625, ((0, 8), (1, 32))),
        "cotangent": noise(streams_of[3], (TOKENS, D), 1.0, 6.0, ((0, 8), (1, 32))),
    }


def slope(hidden):
    normal_cdf = 0.5 * (1.0 + jax.scipy.special.erf(hidden * (1.0 / math.sqrt(2.0))))
    density = jnp.exp(-0.5 * hidden * hidden) * (1.0 / math.sqrt(2.0 * math.pi))
    return normal_cdf + hidden * density

def rounded(term):
    return lax.optimization_barrier(term.astype(jnp.bfloat16)).astype(jnp.float32)

def reference(tokens, first_weight, second_weight, cotangent):
    hidden = jnp.dot(tokens, first_weight, preferred_element_type=jnp.float32)
    active = jax.nn.gelu(hidden, approximate=False).astype(jnp.bfloat16)
    output = jnp.dot(active, second_weight, preferred_element_type=jnp.float32).astype(jnp.bfloat16)
    upward = jnp.dot(cotangent, second_weight.T, preferred_element_type=jnp.float32)
    deltas = (upward * slope(hidden)).astype(jnp.bfloat16)
    input_grad = jnp.dot(deltas, first_weight.T, preferred_element_type=jnp.float32).astype(jnp.bfloat16)
    factor = float(TOKENS) ** (-0.5)
    first_total = jnp.zeros((D, F), jnp.float32)
    second_total = jnp.zeros((F, D), jnp.float32)
    for member in range(N_GRP):
        lower = member * TOK_G
        upper = lower + TOK_G
        first_total = first_total + rounded(factor * jnp.dot(tokens[lower:upper].T, deltas[lower:upper], preferred_element_type=jnp.float32))
        second_total = second_total + rounded(factor * jnp.dot(active[lower:upper].T, cotangent[lower:upper], preferred_element_type=jnp.float32))
    return (output, input_grad, first_total.astype(jnp.bfloat16), second_total.astype(jnp.bfloat16))
```

```python
import math

import jax
import jax.numpy as jnp
from jax import lax
from jax.sharding import PartitionSpec as P

BF = jnp.bfloat16
F32 = jnp.float32
GRP = 8
X, Z, C = 4, 4, 2


def rep_index(x, z, c):
    return (x * Z + z) * C + c


X_GROUPS = [[rep_index(x, z, c) for x in range(X)] for z in range(Z) for c in range(C)]
Z_GROUPS = [[rep_index(x, z, c) for z in range(Z)] for x in range(X) for c in range(C)]
C_GROUPS = [[rep_index(x, z, c) for c in range(C)] for x in range(X) for z in range(Z)]


def slope(hidden):
    normal_cdf = 0.5 * (1.0 + jax.scipy.special.erf(hidden * (1.0 / math.sqrt(2.0))))
    density = jnp.exp(-0.5 * hidden * hidden) * (1.0 / math.sqrt(2.0 * math.pi))
    return normal_cdf + hidden * density


def dot(left, right, dims):
    return lax.dot_general(left, right, (dims, ((), ())), preferred_element_type=F32)


def exchange(value, groups, axis="rep"):
    return lax.all_to_all(value, axis, 0, 0, axis_index_groups=groups)


def scatter_sum(value, groups, axis="rep"):
    return jnp.sum(exchange(value.astype(BF), groups, axis).astype(F32), axis=0)


def gather(value, groups, count, axis="rep"):
    return exchange(jnp.broadcast_to(value[None], (count,) + value.shape), groups, axis)


def body(tokens, first_weight, second_weight, cotangent):
    rows, width = tokens.shape
    hid = first_weight.shape[1]
    total = rows * GRP
    factor = float(total) ** (-0.5)
    part = total // (C * X * Z)

    both = gather(jnp.stack([tokens, cotangent]), None, GRP, "grp")
    tok = both[:, 0].reshape(total, width)
    cot = both[:, 1].reshape(total, width)

    partial_hidden = dot(tok, first_weight, ((1,), (0,)))
    partial_upward = dot(cot, second_weight, ((1,), (1,)))
    sums = jnp.stack(
        [v.reshape(C, X, Z, part, hid) for v in (partial_hidden, partial_upward)], axis=3
    )
    sums = scatter_sum(sums, C_GROUPS)
    sums = scatter_sum(sums, X_GROUPS)
    sums = scatter_sum(sums, Z_GROUPS)
    hidden, upward = sums[0], sums[1]
    active = jax.nn.gelu(hidden, approximate=False).astype(BF)
    deltas = (upward * slope(hidden)).astype(BF)

    acts = jnp.stack([active, deltas])
    acts = gather(acts, Z_GROUPS, Z)
    acts = gather(acts, X_GROUPS, X)
    acts = gather(acts, C_GROUPS, C)
    active = acts[:, :, :, 0].reshape(total, hid)
    deltas = acts[:, :, :, 1].reshape(total, hid)

    out = dot(active, second_weight, ((1,), (0,)))
    back = dot(deltas, first_weight, ((1,), (1,)))
    outs = jnp.stack([v.reshape(GRP, rows, width) for v in (out, back)], axis=1)
    outs = scatter_sum(outs, None, "grp").astype(BF)
    first_grad = (factor * dot(tok, deltas, ((0,), (0,)))).astype(BF)
    second_grad = (factor * dot(active, cot, ((0,), (0,)))).astype(BF)
    return (outs[0], outs[1], first_grad, second_grad)


def solution(mesh):
    in_specs = (P("grp", "rep"), P("rep", "grp"), P("grp", "rep"), P("grp", "rep"))
    out_specs = (P("grp", "rep"), P("grp", "rep"), P("rep", "grp"), P("grp", "rep"))
    return jax.shard_map(body, mesh=mesh, in_specs=in_specs, out_specs=out_specs, check_vma=False)
```

```python
import math

import jax
import jax.numpy as jnp
from jax import lax
from jax.sharding import PartitionSpec as P

BF = jnp.bfloat16
F32 = jnp.float32
X, Y, Z, C = 4, 4, 4, 2


def rep_index(x, z, c):
    return ((x % X) * Z + z % Z) * C + c % C


def grp_index(w, y):
    return (w % 2) * Y + y % Y


def rep_pairs(dx, dz, dc):
    return [
        (rep_index(x, z, c), rep_index(x + dx, z + dz, c + dc))
        for x in range(X)
        for z in range(Z)
        for c in range(C)
    ]


def grp_pairs(dw, dy):
    return [(grp_index(w, y), grp_index(w + dw, y + dy)) for w in range(2) for y in range(Y)]


def move_x(value, d):
    return lax.ppermute(value, "rep", rep_pairs(d, 0, 0))


def move_z(value, d):
    return lax.ppermute(value, "rep", rep_pairs(0, d, 0))


def move_core(value):
    return lax.ppermute(value, "rep", rep_pairs(0, 0, 1))


def move_y(value, d):
    return lax.ppermute(value, "grp", grp_pairs(0, d))


def move_w(value):
    return lax.ppermute(value, "grp", grp_pairs(1, 0))


def after(value, *others):
    return lax.optimization_barrier((value,) + others)[0]


def slope(hidden):
    normal_cdf = 0.5 * (1.0 + jax.scipy.special.erf(hidden * (1.0 / math.sqrt(2.0))))
    density = jnp.exp(-0.5 * hidden * hidden) * (1.0 / math.sqrt(2.0 * math.pi))
    return normal_cdf + hidden * density


def dot(left, right, dims):
    return lax.dot_general(left, right, (dims, ((), ())), preferred_element_type=F32)


def place():
    rep = lax.axis_index("rep")
    return rep >> 3, (rep >> 1) & 3, rep & 1


def roll_rows(value, shift):
    chunks = value.reshape(Z, -1, value.shape[1])
    twice = jnp.concatenate([chunks, chunks])
    return lax.dynamic_slice_in_dim(twice, shift, Z).reshape(value.shape)


def gather_rows(value):
    x, z, c = place()
    value = roll_rows(value, z)
    pair = jnp.stack([value, move_w(value)])
    blocks = [pair] + [move_y(pair, -d) for d in range(1, Y)]
    own = jnp.zeros((X,) + value.shape, BF)
    other = own
    for d, block in enumerate(blocks):
        k = (d - x) & 3
        mine = jnp.where(c == 0, block[0], block[1])
        theirs = jnp.where(c == 0, block[1], block[0])
        own = lax.dynamic_update_slice(own, mine[None], (k, 0, 0))
        other = lax.dynamic_update_slice(other, theirs[None], (k, 0, 0))
    shape = (X * value.shape[0], value.shape[1])
    return own.reshape(shape), other.reshape(shape), blocks[-1]


def sum_partials(own, other, weight, dims):
    theirs = dot(other, weight, dims).astype(BF)
    arrived = move_core(theirs)
    mine = dot(own, weight, dims)
    total = (mine + arrived.astype(F32)).reshape(X, -1, mine.shape[1])
    sent = total.astype(BF)
    arrived = [move_x(sent[d], d) for d in range(1, X)]
    total = total[0]
    for block in arrived:
        total = total + block.astype(F32)
    total = total.reshape(Z, -1, total.shape[1])
    sent = total.astype(BF)
    arrived = [move_z(sent[d], d) for d in range(1, Z)]
    total = total[0]
    for block in arrived:
        total = total + block.astype(F32)
    return total


def spread(value):
    block = jnp.concatenate([value] + [move_z(value, -d) for d in range(1, Z)])
    half = jnp.concatenate([block] + [move_x(block, -d) for d in range(1, X)])
    return half, move_core(half)


def sum_rows(own, other):
    x, z, c = place()
    own = own.reshape(X, -1, own.shape[1])
    other = other.reshape(own.shape)
    first = jnp.where(c == 0, own, other)
    second = jnp.where(c == 0, other, own)
    both = jnp.stack([first, second], axis=1)
    sent = both.astype(BF)
    total = lax.dynamic_index_in_dim(both, (0 - x) & 3, keepdims=False)
    for d in range(1, Y):
        block = lax.dynamic_index_in_dim(sent, (d - x) & 3, keepdims=False)
        total = total + move_y(block, d).astype(F32)
    total = total[0] + move_w(total[1].astype(BF)).astype(F32)
    return roll_rows(total, (0 - z) & 3).astype(BF)


def body(tokens, first_weight, second_weight, cotangent):
    factor = float(tokens.shape[0] * lax.axis_size("grp")) ** (-0.5)
    tok, tok_other, last = gather_rows(tokens)
    cotangent = after(cotangent, last)
    cot, cot_other, _ = gather_rows(cotangent)

    hidden = sum_partials(tok, tok_other, first_weight, ((1,), (0,)))
    active = jax.nn.gelu(hidden, approximate=False).astype(BF)
    active, hidden = lax.optimization_barrier((active, hidden))
    upward = sum_partials(cot, cot_other, second_weight, ((1,), (1,)))
    deltas = after((upward * slope(hidden)).astype(BF))

    act, act_other = spread(active)
    dlt, dlt_other = spread(deltas)

    out = sum_rows(
        dot(act, second_weight, ((1,), (0,))), dot(act_other, second_weight, ((1,), (0,)))
    )
    back = sum_rows(
        dot(dlt, first_weight, ((1,), (1,))), dot(dlt_other, first_weight, ((1,), (1,)))
    )
    rows = ((0,), (0,))
    second_grad = (factor * (dot(act, cot, rows) + dot(act_other, cot_other, rows))).astype(BF)
    first_grad = (factor * (dot(tok, dlt, rows) + dot(tok_other, dlt_other, rows))).astype(BF)
    return (out, back, first_grad, second_grad)


def solution(mesh):
    in_specs = (P("grp", "rep"), P("rep", "grp"), P("grp", "rep"), P("grp", "rep"))
    out_specs = (P("grp", "rep"), P("grp", "rep"), P("rep", "grp"), P("grp", "rep"))
    return jax.shard_map(body, mesh=mesh, in_specs=in_specs, out_specs=out_specs, check_vma=False)
```

```python
import math

import jax
import jax.numpy as jnp
from jax import lax
from jax.experimental import pallas as pl
from jax.experimental.pallas import tpu as pltpu
from jax.sharding import PartitionSpec as P

BF = jnp.bfloat16
F32 = jnp.float32
X, Y, Z, C = 4, 4, 4, 2


def rep_index(x, z, c):
    return ((x % X) * Z + z % Z) * C + c % C


def grp_index(w, y):
    return (w % 2) * Y + y % Y


def rep_pairs(dx, dz, dc):
    return [
        (rep_index(x, z, c), rep_index(x + dx, z + dz, c + dc))
        for x in range(X)
        for z in range(Z)
        for c in range(C)
    ]


def grp_pairs(dw, dy):
    return [(grp_index(w, y), grp_index(w + dw, y + dy)) for w in range(2) for y in range(Y)]


def move_x(value, d):
    return lax.ppermute(value, "rep", rep_pairs(d, 0, 0))


def move_z(value, d):
    return lax.ppermute(value, "rep", rep_pairs(0, d, 0))


def move_core(value):
    return lax.ppermute(value, "rep", rep_pairs(0, 0, 1))


def move_y(value, d):
    return lax.ppermute(value, "grp", grp_pairs(0, d))


def move_w(value):
    return lax.ppermute(value, "grp", grp_pairs(1, 0))


def after(value, *others):
    return lax.optimization_barrier((value,) + others)[0]


def slope(hidden):
    normal_cdf = 0.5 * (1.0 + jax.scipy.special.erf(hidden * (1.0 / math.sqrt(2.0))))
    density = jnp.exp(-0.5 * hidden * hidden) * (1.0 / math.sqrt(2.0 * math.pi))
    return normal_cdf + hidden * density


def dot(left, right, dims):
    return lax.dot_general(left, right, (dims, ((), ())), preferred_element_type=F32)


def position():
    rep = lax.axis_index("rep")
    return jnp.stack([rep >> 3, (rep >> 1) & 3, rep & 1]).astype(jnp.int32)


def kernel_call(kernel, outs, scratch, flops, *operands):
    moved = sum(math.prod(o.shape) * o.dtype.itemsize for o in operands + tuple(outs))
    vmem = pl.BlockSpec(memory_space=pltpu.VMEM)
    return pl.pallas_call(
        kernel,
        out_shape=outs,
        in_specs=[pl.BlockSpec(memory_space=pltpu.SMEM)] + [vmem] * (len(operands) - 1),
        out_specs=[vmem] * len(outs),
        scratch_shapes=scratch,
        compiler_params=pltpu.CompilerParams(vmem_limit_bytes=24 * 1024 * 1024),
        cost_estimate=pl.CostEstimate(flops=flops, bytes_accessed=moved, transcendentals=0),
    )(*operands)


def shaped(shape, dtype):
    return jax.ShapeDtypeStruct(shape, dtype)


def roll_rows(value, shift):
    chunks = value.reshape(Z, -1, value.shape[1])
    twice = jnp.concatenate([chunks, chunks])
    return lax.dynamic_slice_in_dim(twice, shift, Z).reshape(value.shape)


def row_of(value):
    return [value] + [move_y(value, -d) for d in range(1, Y)]


def first_product(pos, blocks, weight, dims, hid):
    rows, width = blocks[0].shape

    def kernel(pos_ref, *refs):
        weight_ref, own_ref, other_ref, sent_ref = refs[-4:]
        x, c = pos_ref[0], pos_ref[2]
        for index in range(2 * Y):
            dz, dy = divmod(index, Y)
            k = (dy - x) & 3

            @pl.when(c == dz)
            def _():
                own_ref[k] = refs[index][...]

            @pl.when(c != dz)
            def _():
                other_ref[k] = refs[index][...]

        for k in range(X):
            here = pl.ds(k * rows, rows)
            sent_ref[here, lanes - 128 :] = jnp.zeros((rows, 128), BF)
            sent_ref[here, :hid] = dot(other_ref[k], weight_ref[...], dims).astype(BF)

    lanes = -(-hid // 128) * 128
    half = shaped((X, rows, width), BF)
    flops = 2 * X * rows * width * hid
    outs = [half, half, shaped((X * rows, lanes), BF)]
    return kernel_call(kernel, outs, [], flops, pos, *blocks, weight)


def second_product(pos, own, arrived, weight, dims):
    _, rows, width = own.shape
    hid = weight.shape[1 - dims[1][0]]

    def kernel(pos_ref, own_ref, arrived_ref, weight_ref, keep_ref, *sent):
        for k in range(X):
            total = dot(own_ref[k], weight_ref[...], dims)
            total = total + arrived_ref[pl.ds(k * rows, rows), :hid].astype(F32)
            if k == 0:
                keep_ref[...] = total
            else:
                sent[k - 1][...] = total.astype(BF)

    flops = 2 * X * rows * width * hid
    outs = [shaped((rows, hid), F32)] + [shaped((rows, hid), BF)] * (X - 1)
    return kernel_call(kernel, outs, [], flops, pos, own, arrived, weight)


def last_product(pos, blocks, weight, dims, width):
    rows, hid = blocks[0].shape

    def kernel(pos_ref, *refs):
        blocks_ref, weight_ref = refs[: 2 * X], refs[2 * X]
        all_ref, keep0_ref, keep1_ref = refs[2 * X + 1 : 2 * X + 4]
        sent, total_ref = refs[2 * X + 4 : -1], refs[-1]
        x, c = pos_ref[0], pos_ref[2]
        for index in range(2 * X):
            h, k = divmod(index, X)
            block = blocks_ref[index][...]
            all_ref[index] = block
            total_ref[(c ^ h) * Y + ((x + k) & 3)] = dot(block, weight_ref[...], dims)
        keep0_ref[...] = total_ref[0]
        keep1_ref[...] = total_ref[Y]
        for d in range(1, Y):
            sent[d - 1][...] = total_ref[d].astype(BF)
            sent[Y - 2 + d][...] = total_ref[Y + d].astype(BF)

    flops = 2 * 2 * X * rows * width * hid
    outs = [shaped((2 * X, rows, hid), BF)]
    outs += [shaped((rows, width), F32)] * 2
    outs += [shaped((rows, width), BF)] * (2 * (Y - 1))
    scratch = [pltpu.VMEM((2 * Y, rows, width), F32)]
    return kernel_call(kernel, outs, scratch, flops, pos, *blocks, weight)


def add_all(keep, arrived):
    for block in arrived:
        keep = keep + block.astype(F32)
    return keep


def sum_x(keep, sent):
    arrived = [move_x(sent[d - 1], d) for d in range(1, X)]
    arrived = list(lax.optimization_barrier(tuple(arrived)))
    total = add_all(keep, arrived)
    total = total.reshape(Z, -1, total.shape[1])
    return total[0], [total[d].astype(BF) for d in range(1, Z)]


def sum_z(keep, sent):
    return add_all(keep, [move_z(sent[d - 1], d) for d in range(1, Z)])


def spread(value):
    block = jnp.concatenate([value] + [move_z(value, -d) for d in range(1, Z)])
    half = [block] + [move_x(block, -d) for d in range(1, X)]
    return half + [move_core(part) for part in half]


def sum_groups(pos, keep0, keep1, sent):
    far = add_all(keep1, [move_y(sent[Y - 2 + d], d) for d in range(1, Y)])
    far = move_w(far.astype(BF))
    near = add_all(keep0, [move_y(sent[d - 1], d) for d in range(1, Y)])
    return roll_rows(near + far.astype(F32), (0 - pos[1]) & 3).astype(BF)


def body(tokens, first_weight, second_weight, cotangent):
    width, hid = first_weight.shape
    total = 2 * Y * tokens.shape[0]
    factor = float(total) ** (-0.5)
    pos = position()

    tok = row_of(roll_rows(tokens, pos[1]))
    tok += row_of(move_w(tok[0]))
    cotangent = after(cotangent, tok[1])
    cot = row_of(roll_rows(cotangent, pos[1]))
    partner = move_w(cot[0])

    tok, tok_other, sent = first_product(pos, tok, first_weight, ((1,), (0,)), hid)
    sent = after(move_core(sent), *cot[1:])
    keep, *sent = second_product(pos, tok, sent, first_weight, ((1,), (0,)))
    cot += row_of(after(partner, keep))
    keep, sent = sum_x(keep, sent)
    cot[0] = after(cot[0], *sent)
    hidden = sum_z(keep, sent)
    active = jax.nn.gelu(hidden, approximate=False).astype(BF)
    active, hidden = lax.optimization_barrier((active, hidden))

    cot, cot_other, sent = first_product(pos, cot, second_weight, ((1,), (1,)), hid)
    keep, *sent = second_product(pos, cot, move_core(sent), second_weight, ((1,), (1,)))
    keep, sent = sum_x(keep, sent)
    upward = sum_z(keep, sent)
    deltas = after((upward * slope(hidden)).astype(BF))

    act, *outs = last_product(pos, spread(active), second_weight, ((1,), (0,)), width)
    out = sum_groups(pos, *outs[:2], outs[2:])
    dlt, *outs = last_product(pos, spread(deltas), first_weight, ((1,), (1,)), width)
    back = sum_groups(pos, *outs[:2], outs[2:])

    act, dlt = act.reshape(total, hid), dlt.reshape(total, hid)
    tok = jnp.concatenate([tok, tok_other]).reshape(total, width)
    cot = jnp.concatenate([cot, cot_other]).reshape(total, width)
    second_grad = (factor * dot(act, cot, ((0,), (0,)))).astype(BF)
    first_grad = (factor * dot(tok, dlt, ((0,), (0,)))).astype(BF)
    return (out, back, first_grad, second_grad)


def solution(mesh):
    in_specs = (P("grp", "rep"), P("rep", "grp"), P("grp", "rep"), P("grp", "rep"))
    out_specs = (P("grp", "rep"), P("grp", "rep"), P("rep", "grp"), P("grp", "rep"))
    return jax.shard_map(body, mesh=mesh, in_specs=in_specs, out_specs=out_specs, check_vma=False)
```

```python
import math

import jax
import jax.numpy as jnp
from jax import lax
from jax.experimental import pallas as pl
from jax.experimental.pallas import tpu as pltpu
from jax.sharding import PartitionSpec as P

BF = jnp.bfloat16
F32 = jnp.float32
GRP = 8
X, Z, C = 4, 4, 2
LANES = 128


def rep_index(x, z, c):
    return (x * Z + z) * C + c


def rep_pairs(dx, dc):
    return [
        (rep_index(x, z, c), rep_index((x + dx) % X, z, (c + dc) % C))
        for x in range(X)
        for z in range(Z)
        for c in range(C)
    ]


Z_GROUPS = [[rep_index(x, z, c) for z in range(Z)] for x in range(X) for c in range(C)]


def after(value, *others):
    return lax.optimization_barrier((value,) + others)[0]


def slope(hidden):
    normal_cdf = 0.5 * (1.0 + jax.scipy.special.erf(hidden * (1.0 / math.sqrt(2.0))))
    density = jnp.exp(-0.5 * hidden * hidden) * (1.0 / math.sqrt(2.0 * math.pi))
    return normal_cdf + hidden * density


def dot(left, right, dims):
    return lax.dot_general(left, right, (dims, ((), ())), preferred_element_type=F32)


PLAIN = ((1,), (0,))
LAST = ((1,), (1,))


def shaped(shape, dtype):
    return jax.ShapeDtypeStruct(shape, dtype)


def kernel_call(kernel, outs, flops, pos, operands, scratch=()):
    moved = sum(math.prod(o.shape) * o.dtype.itemsize for o in [*operands, *outs])
    vmem = pl.BlockSpec(memory_space=pltpu.VMEM)
    return pl.pallas_call(
        kernel,
        out_shape=outs,
        in_specs=[pl.BlockSpec(memory_space=pltpu.SMEM)] + [vmem] * len(operands),
        out_specs=[vmem] * len(outs),
        scratch_shapes=scratch,
        compiler_params=pltpu.CompilerParams(vmem_limit_bytes=24 * 1024 * 1024),
        cost_estimate=pl.CostEstimate(flops=flops, bytes_accessed=moved, transcendentals=0),
    )(pos, *operands)


def half_of(ref, half, x):
    return jnp.concatenate([ref[half * X + ((x + d) & 3)] for d in range(X)], axis=1)


def wide(refs):
    return jnp.concatenate([ref[...] for ref in refs], axis=1)


def block(value, d):
    return value[:, d * LANES : (d + 1) * LANES]


def other_half(pos, rows, weight):
    depth, width = weight.shape

    def kernel(pos_ref, rows_ref, weight_ref, out_ref):
        rows = half_of(rows_ref, 1 - pos_ref[1], pos_ref[0])
        product = dot(weight_ref[...], rows, PLAIN).astype(BF)
        for d in range(X):
            out_ref[d] = block(product, d)

    outs = [shaped((X, depth, LANES), BF)]
    return kernel_call(kernel, outs, 2 * depth * width * X * LANES, pos, [rows, weight])[0]


def own_half(pos, rows, weight, arrived):
    depth, width = weight.shape

    def kernel(pos_ref, rows_ref, weight_ref, arrived_ref, keep_ref, *sent):
        product = dot(weight_ref[...], half_of(rows_ref, pos_ref[1], pos_ref[0]), PLAIN)
        for d in range(X):
            total = block(product, d) + arrived_ref[d].astype(F32)
            if d == 0:
                keep_ref[...] = total
            else:
                sent[d - 1][...] = total.astype(BF)

    outs = [shaped((depth, LANES), F32)] + [shaped((depth, LANES), BF)] * (X - 1)
    flops = 2 * depth * width * X * LANES
    keep, *sent = kernel_call(kernel, outs, flops, pos, [rows, weight, arrived])
    return keep, sent


def both_halves(pos, blocks, weight):
    depth, width = weight.shape

    def kernel(pos_ref, *refs):
        weight_ref, out_ref = refs[-2:]
        x, c = pos_ref[0], pos_ref[1]
        for part, half in ((refs[:X], c), (refs[X : 2 * X], 1 - c)):
            product = dot(weight_ref[...], wide(part), PLAIN).astype(BF)
            for d in range(X):
                out_ref[half * X + ((x + d) & 3)] = block(product, d)

    outs = [shaped((2 * X, depth, LANES), BF)]
    flops = 2 * depth * width * 2 * X * LANES
    return kernel_call(kernel, outs, flops, pos, [*blocks, weight])[0]


def weight_grad(pos, factor, rows, blocks, rows_first):
    width, depth = rows.shape[1], blocks[0].shape[0]

    def kernel(pos_ref, rows_ref, *refs):
        out_ref, total = refs[-1], None
        x, c = pos_ref[0], pos_ref[1]
        for part, half in ((refs[:X], c), (refs[X : 2 * X], 1 - c)):
            pair = half_of(rows_ref, half, x), wide(part)
            term = dot(*(pair if rows_first else pair[::-1]), LAST)
            total = term if total is None else total + term
        out_ref[...] = (factor * total).astype(BF)

    outs = [shaped((width, depth) if rows_first else (depth, width), BF)]
    flops = 2 * depth * width * 2 * X * LANES
    return kernel_call(kernel, outs, flops, pos, [rows, *blocks])[0]


def exchange(value, axis, groups=None):
    return lax.all_to_all(value, axis, 0, 0, axis_index_groups=groups)


def copies(value, count):
    return jnp.broadcast_to(value[None], (count,) + value.shape)


def swap_cores(value):
    return lax.ppermute(value, "rep", rep_pairs(0, 1))


def move_x(value, d):
    return lax.ppermute(value, "rep", rep_pairs(d, 0))


def total_of(value):
    return jnp.sum(value.astype(F32), axis=0)


def sum_x(keep, sent):
    arrived = lax.optimization_barrier(tuple(move_x(sent[d - 1], d) for d in range(1, X)))
    for part in arrived:
        keep = keep + part.astype(F32)
    return keep.astype(BF)


def sum_z(value):
    value = value.reshape(Z, value.shape[0] // Z, LANES)
    return total_of(exchange(value, "rep", Z_GROUPS))


def spread_z(value):
    whole = exchange(copies(value, Z), "rep", Z_GROUPS)
    return whole.reshape(Z * value.shape[0], LANES)


def spread_x(value):
    own = [value] + [move_x(value, -d) for d in range(1, X)]
    return own + [swap_cores(part) for part in own]


def body(tokens, first_weight, second_weight, cotangent):
    factor = float(GRP * tokens.shape[0]) ** (-0.5)
    rep = lax.axis_index("rep")
    pos = jnp.stack([rep >> 3, rep & 1]).astype(jnp.int32)

    tok = exchange(copies(tokens.T, GRP), "grp")
    first_turned, second_turned = first_weight.T, second_weight.T
    sent = other_half(pos, tok, first_turned)
    cot = exchange(copies(after(cotangent.T, sent), GRP), "grp")
    keep, sent = own_half(pos, tok, first_turned, swap_cores(sent))
    value = sum_x(keep, sent)
    hidden = sum_z(value)
    active = jax.nn.gelu(hidden, approximate=False).astype(BF)
    active, hidden = lax.optimization_barrier((active, hidden))

    sent = other_half(pos, after(cot, value), second_weight)
    keep, sent = own_half(pos, cot, second_weight, swap_cores(sent))
    upward = sum_z(sum_x(keep, sent))
    deltas = (upward * slope(hidden)).astype(BF)

    act = spread_x(spread_z(active))
    dlt = spread_x(spread_z(deltas))
    out = exchange(both_halves(pos, act, second_turned), "grp")
    back = exchange(both_halves(pos, dlt, first_weight), "grp")
    second_grad = weight_grad(pos, factor, cot, act, False)
    first_grad = weight_grad(pos, factor, tok, dlt, True)
    return (total_of(out).astype(BF).T, total_of(back).astype(BF).T, first_grad, second_grad)


def solution(mesh):
    in_specs = (P("grp", "rep"), P("rep", "grp"), P("grp", "rep"), P("grp", "rep"))
    out_specs = (P("grp", "rep"), P("grp", "rep"), P("rep", "grp"), P("grp", "rep"))
    return jax.shard_map(body, mesh=mesh, in_specs=in_specs, out_specs=out_specs, check_vma=False)
```

```python
import math

import jax
import jax.numpy as jnp
from jax import lax
from jax.experimental import pallas as pl
from jax.experimental.pallas import tpu as pltpu
from jax.sharding import PartitionSpec as P

BF = jnp.bfloat16
F32 = jnp.float32
GRP = 8
X, Z, C = 4, 4, 2
LANES = 128


def rep_index(x, z, c):
    return (x * Z + z) * C + c


def rep_pairs(dx, dz, dc):
    return [
        (rep_index(x, z, c), rep_index((x + dx) % X, (z + dz) % Z, (c + dc) % C))
        for x in range(X)
        for z in range(Z)
        for c in range(C)
    ]


Z_GROUPS = [[rep_index(x, z, c) for z in range(Z)] for x in range(X) for c in range(C)]


def after(value, *others):
    return lax.optimization_barrier((value,) + others)[0]


def slope(hidden):
    normal_cdf = 0.5 * (1.0 + jax.scipy.special.erf(hidden * (1.0 / math.sqrt(2.0))))
    density = jnp.exp(-0.5 * hidden * hidden) * (1.0 / math.sqrt(2.0 * math.pi))
    return normal_cdf + hidden * density


def dot(left, right, dims):
    return lax.dot_general(left, right, (dims, ((), ())), preferred_element_type=F32)


PLAIN = ((1,), (0,))
LAST = ((1,), (1,))


def shaped(shape, dtype):
    return jax.ShapeDtypeStruct(shape, dtype)


def kernel_call(kernel, outs, flops, pos, operands, scratch=(), far=()):
    moved = sum(math.prod(o.shape) * o.dtype.itemsize for o in [*operands, *outs])
    vmem = pl.BlockSpec(memory_space=pltpu.VMEM)
    return pl.pallas_call(
        kernel,
        out_shape=[pltpu.HBM(o.shape, o.dtype) if i in far else o for i, o in enumerate(outs)],
        in_specs=[pl.BlockSpec(memory_space=pltpu.SMEM)] + [vmem] * len(operands),
        out_specs=[
            pl.BlockSpec(memory_space=pltpu.HBM) if i in far else vmem for i in range(len(outs))
        ],
        scratch_shapes=scratch,
        compiler_params=pltpu.CompilerParams(vmem_limit_bytes=16 * 1024 * 1024),
        cost_estimate=pl.CostEstimate(flops=flops, bytes_accessed=moved, transcendentals=0),
    )(pos, *operands)


def half_of(ref, half, x):
    return jnp.concatenate([ref[half * X + ((x + d) & 3)] for d in range(X)], axis=1)


def wide(refs):
    return jnp.concatenate([ref[...] for ref in refs], axis=1)


def block(value, d):
    return value[:, d * LANES : (d + 1) * LANES]


def other_half(pos, rows, weight):
    depth, width = weight.shape

    def kernel(pos_ref, rows_ref, weight_ref, out_ref):
        rows = half_of(rows_ref, 1 - pos_ref[1], pos_ref[0])
        product = dot(weight_ref[...], rows, PLAIN).astype(BF)
        for d in range(X):
            out_ref[d] = block(product, d)

    outs = [shaped((X, depth, LANES), BF)]
    return kernel_call(kernel, outs, 2 * depth * width * X * LANES, pos, [rows, weight])[0]


def own_half(pos, rows, weight, arrived):
    depth, width = weight.shape

    def kernel(pos_ref, rows_ref, weight_ref, arrived_ref, keep_ref, *sent):
        product = dot(weight_ref[...], half_of(rows_ref, pos_ref[1], pos_ref[0]), PLAIN)
        for d in range(X):
            total = block(product, d) + arrived_ref[d].astype(F32)
            if d == 0:
                keep_ref[...] = total
            else:
                sent[d - 1][...] = total.astype(BF)

    outs = [shaped((depth, LANES), F32)] + [shaped((depth, LANES), BF)] * (X - 1)
    flops = 2 * depth * width * X * LANES
    keep, *sent = kernel_call(kernel, outs, flops, pos, [rows, weight, arrived])
    return keep, sent


def both_halves(pos, blocks, weight):
    depth, width = weight.shape
    count = 2 * X

    def kernel(pos_ref, *refs):
        weight_ref, out_ref, kept_ref, sems = refs[-4:]
        kept = [
            pltpu.make_async_copy(refs[index], kept_ref.at[index], sems.at[index])
            for index in range(count)
        ]
        for copy in kept:
            copy.start()
        x, c = pos_ref[0], pos_ref[1]
        for part, half in ((refs[:X], c), (refs[X:count], 1 - c)):
            product = dot(weight_ref[...], wide(part), PLAIN).astype(BF)
            for d in range(X):
                out_ref[half * X + ((x + d) & 3)] = block(product, d)
        for copy in kept:
            copy.wait()

    outs = [shaped((count, depth, LANES), BF), shaped((count, width, LANES), BF)]
    flops = 2 * depth * width * count * LANES
    scratch = [pltpu.SemaphoreType.DMA((count,))]
    return kernel_call(kernel, outs, flops, pos, [*blocks, weight], scratch, (1,))


def weight_grad(pos, factor, rows, blocks, rows_first):
    width, depth = rows.shape[1], blocks.shape[1]

    def kernel(pos_ref, rows_ref, blocks_ref, out_ref):
        x, c = pos_ref[0], pos_ref[1]
        total = None
        for part, half in ((0, c), (1, 1 - c)):
            pair = half_of(rows_ref, half, x), half_of(blocks_ref, part, 0)
            term = dot(*(pair if rows_first else pair[::-1]), LAST)
            total = term if total is None else total + term
        out_ref[...] = (factor * total).astype(BF)

    outs = [shaped((width, depth) if rows_first else (depth, width), BF)]
    flops = 2 * depth * width * 2 * X * LANES
    return kernel_call(kernel, outs, flops, pos, [rows, blocks])[0]


def exchange(value, axis, groups=None):
    return lax.all_to_all(value, axis, 0, 0, axis_index_groups=groups)


def copies(value, count):
    return jnp.broadcast_to(value[None], (count,) + value.shape)


def many(pos, value, count):
    def kernel(pos_ref, value_ref, out_ref):
        for index in range(count):
            out_ref[index] = value_ref[...]

    return kernel_call(kernel, [shaped((count,) + value.shape, BF)], 0, pos, [value])[0]


def added(pos, value):
    def kernel(pos_ref, value_ref, out_ref):
        total = value_ref[0].astype(F32)
        for index in range(1, value.shape[0]):
            total = total + value_ref[index].astype(F32)
        out_ref[...] = total.astype(BF)

    return kernel_call(kernel, [shaped(value.shape[1:], BF)], value.size, pos, [value])[0]


def in_order(pos, chunks):
    def kernel(pos_ref, *refs):
        for d in range(Z):
            refs[-1][(pos_ref[2] + d) & 3] = refs[d][...]

    return kernel_call(kernel, [shaped((Z,) + chunks[0].shape, BF)], 0, pos, chunks)[0]


def swap_cores(value):
    return lax.ppermute(value, "rep", rep_pairs(0, 0, 1))


def move_x(value, d):
    return lax.ppermute(value, "rep", rep_pairs(d, 0, 0))


def move_z(value, d):
    return lax.ppermute(value, "rep", rep_pairs(0, d, 0))


def total_of(value):
    return jnp.sum(value.astype(F32), axis=0)


def sum_x(keep, sent):
    arrived = lax.optimization_barrier(tuple(move_x(sent[d - 1], d) for d in range(1, X)))
    for part in arrived:
        keep = keep + part.astype(F32)
    return keep.astype(BF)


def scatter_z(value):
    value = value.reshape(Z, value.shape[0] // Z, LANES)
    return exchange(value, "rep", Z_GROUPS)


def spread_z(pos, value, by_permutes):
    if by_permutes:
        whole = in_order(pos, [value] + [move_z(value, -d) for d in range(1, Z)])
    else:
        whole = exchange(copies(value, Z), "rep", Z_GROUPS)
    return whole.reshape(Z * value.shape[0], LANES)


def spread_x(value):
    own = [value] + [move_x(value, -d) for d in range(1, X)]
    return own + [swap_cores(part) for part in own]


def body(tokens, first_weight, second_weight, cotangent):
    factor = float(GRP * tokens.shape[0]) ** (-0.5)
    rep = lax.axis_index("rep")
    pos = jnp.stack([rep >> 3, rep & 1, (rep >> 1) & 3]).astype(jnp.int32)

    tok = exchange(many(pos, tokens.T, GRP), "grp")
    first_turned, second_turned, tok = lax.optimization_barrier(
        (first_weight.T, second_weight.T, tok)
    )
    sent = other_half(pos, tok, first_turned)
    cot = exchange(many(pos, after(cotangent.T, sent), GRP), "grp")
    keep, sent = own_half(pos, tok, first_turned, swap_cores(sent))
    value = sum_x(keep, sent)

    sent = other_half(pos, after(cot, value), second_weight)
    keep, sent = own_half(pos, cot, second_weight, swap_cores(sent))

    hidden = total_of(after(scatter_z(value), keep))
    active = jax.nn.gelu(hidden, approximate=False).astype(BF)
    active, hidden = lax.optimization_barrier((active, hidden))
    upward = total_of(scatter_z(sum_x(keep, sent)))
    deltas = (upward * slope(hidden)).astype(BF)

    act = spread_x(spread_z(pos, active, True))
    dlt = spread_x(spread_z(pos, deltas, False))
    out, act = both_halves(pos, act, second_turned)
    out = exchange(out, "grp")
    second_grad = weight_grad(pos, factor, cot, act, False)
    dlt[0] = after(dlt[0], second_grad)
    back, dlt = both_halves(pos, dlt, first_weight)
    back = exchange(back, "grp")
    first_grad = weight_grad(pos, factor, tok, dlt, True)
    return (added(pos, out).T, added(pos, back).T, first_grad, second_grad)


def solution(mesh):
    in_specs = (P("grp", "rep"), P("rep", "grp"), P("grp", "rep"), P("grp", "rep"))
    out_specs = (P("grp", "rep"), P("grp", "rep"), P("rep", "grp"), P("grp", "rep"))
    return jax.shard_map(body, mesh=mesh, in_specs=in_specs, out_specs=out_specs, check_vma=False)
```

```python
import math

import jax
import jax.numpy as jnp
from jax import lax
from jax.experimental import pallas as pl
from jax.experimental.pallas import tpu as pltpu
from jax.sharding import PartitionSpec as P

BF = jnp.bfloat16
F32 = jnp.float32
GRP = 8
X, Z, C = 4, 4, 2
LANES = 128


def rep_index(x, z, c):
    return (x * Z + z) * C + c


def rep_pairs(dx, dz, dc):
    return [
        (rep_index(x, z, c), rep_index((x + dx) % X, (z + dz) % Z, (c + dc) % C))
        for x in range(X)
        for z in range(Z)
        for c in range(C)
    ]


Z_GROUPS = [[rep_index(x, z, c) for z in range(Z)] for x in range(X) for c in range(C)]


def after(value, *others):
    return lax.optimization_barrier((value,) + others)[0]


def slope(hidden):
    normal_cdf = 0.5 * (1.0 + jax.scipy.special.erf(hidden * (1.0 / math.sqrt(2.0))))
    density = jnp.exp(-0.5 * hidden * hidden) * (1.0 / math.sqrt(2.0 * math.pi))
    return normal_cdf + hidden * density


def dot(left, right, dims):
    return lax.dot_general(left, right, (dims, ((), ())), preferred_element_type=F32)


PLAIN = ((1,), (0,))
LAST = ((1,), (1,))


def shaped(shape, dtype):
    return jax.ShapeDtypeStruct(shape, dtype)


def kernel_call(kernel, outs, flops, pos, operands, scratch=(), far=(), far_in=()):
    moved = sum(math.prod(o.shape) * o.dtype.itemsize for o in [*operands, *outs])
    vmem = pl.BlockSpec(memory_space=pltpu.VMEM)
    hbm = pl.BlockSpec(memory_space=pltpu.HBM)
    return pl.pallas_call(
        kernel,
        out_shape=[pltpu.HBM(o.shape, o.dtype) if i in far else o for i, o in enumerate(outs)],
        in_specs=[pl.BlockSpec(memory_space=pltpu.SMEM)]
        + [hbm if i in far_in else vmem for i in range(len(operands))],
        out_specs=[hbm if i in far else vmem for i in range(len(outs))],
        scratch_shapes=scratch,
        compiler_params=pltpu.CompilerParams(vmem_limit_bytes=16 * 1024 * 1024),
        cost_estimate=pl.CostEstimate(flops=flops, bytes_accessed=moved, transcendentals=0),
    )(pos, *operands)


def half_of(ref, half, x):
    return jnp.concatenate([ref[half * X + ((x + d) & 3)] for d in range(X)], axis=1)


def wide(refs):
    return jnp.concatenate([ref[...] for ref in refs], axis=1)


def block(value, d):
    return value[:, d * LANES : (d + 1) * LANES]


def staged(out):
    return [pltpu.VMEM(out.shape, out.dtype), pltpu.SemaphoreType.DMA(out.shape[:1])]


def other_half(pos, rows, weight):
    depth, width = weight.shape

    def kernel(pos_ref, rows_ref, weight_ref, out_ref, held_ref, sems):
        rows = half_of(rows_ref, 1 - pos_ref[1], pos_ref[0])
        copies = []
        for pair in range(X // 2):
            here = rows[:, pair * 2 * LANES : (pair + 1) * 2 * LANES]
            product = dot(weight_ref[...], here, PLAIN).astype(BF)
            for d in range(2):
                index = pair * 2 + d
                held_ref[index] = block(product, d)
                copies.append(
                    pltpu.make_async_copy(held_ref.at[index], out_ref.at[index], sems.at[index])
                )
                copies[-1].start()
        for copy in copies:
            copy.wait()

    out = shaped((X, depth, LANES), BF)
    flops = 2 * depth * width * X * LANES
    return kernel_call(kernel, [out], flops, pos, [rows, weight], staged(out), (0,))[0]


def own_half(pos, rows, weight, arrived):
    depth, width = weight.shape

    def kernel(pos_ref, rows_ref, weight_ref, arrived_ref, keep_ref, *refs):
        sent, held_ref, sems = refs[: X - 1], refs[-2], refs[-1]
        rows = half_of(rows_ref, pos_ref[1], pos_ref[0])
        copies = []
        for pair in (1, 0):
            here = rows[:, pair * 2 * LANES : (pair + 1) * 2 * LANES]
            product = dot(weight_ref[...], here, PLAIN)
            for i in range(2):
                d = pair * 2 + i
                total = block(product, i) + arrived_ref[d].astype(F32)
                if d == 0:
                    keep_ref[...] = total
                    continue
                held_ref[d - 1] = total.astype(BF)
                copies.append(
                    pltpu.make_async_copy(held_ref.at[d - 1], sent[d - 1], sems.at[d - 1])
                )
                copies[-1].start()
        for copy in copies:
            copy.wait()

    part = shaped((depth, LANES), BF)
    outs = [shaped((depth, LANES), F32)] + [part] * (X - 1)
    scratch = staged(shaped((X - 1,) + part.shape, BF))
    flops = 2 * depth * width * X * LANES
    operands = [rows, weight, arrived]
    keep, *sent = kernel_call(kernel, outs, flops, pos, operands, scratch, range(1, X))
    return keep, sent


def both_halves(pos, blocks, weight):
    depth, width = weight.shape
    count = 2 * X

    def kernel(pos_ref, *refs):
        weight_ref, out_ref, kept_ref, held_ref, out_sems, sems = refs[-6:]
        kept = [
            pltpu.make_async_copy(refs[index], kept_ref.at[index], sems.at[index])
            for index in range(count)
        ]
        for copy in kept:
            copy.start()
        x, c = pos_ref[0], pos_ref[1]
        for part, half in ((refs[:X], c), (refs[X:count], 1 - c)):
            product = dot(weight_ref[...], wide(part), PLAIN).astype(BF)
            for d in range(X):
                index, target = len(kept) - count, half * X + ((x + d) & 3)
                held_ref[index] = block(product, d)
                kept.append(
                    pltpu.make_async_copy(held_ref.at[index], out_ref.at[target], out_sems.at[index])
                )
                kept[-1].start()
        for copy in kept:
            copy.wait()

    outs = [shaped((count, depth, LANES), BF), shaped((count, width, LANES), BF)]
    flops = 2 * depth * width * count * LANES
    scratch = staged(outs[0]) + [pltpu.SemaphoreType.DMA((count,))]
    return kernel_call(kernel, outs, flops, pos, [*blocks, weight], scratch, (0, 1))


def weight_grad(pos, factor, rows, blocks, rows_first):
    width, depth = rows.shape[1], blocks.shape[1]

    def kernel(pos_ref, rows_ref, blocks_ref, out_ref):
        x, c = pos_ref[0], pos_ref[1]
        total = None
        for part, half in ((0, c), (1, 1 - c)):
            pair = half_of(rows_ref, half, x), half_of(blocks_ref, part, 0)
            term = dot(*(pair if rows_first else pair[::-1]), LAST)
            total = term if total is None else total + term
        out_ref[...] = (factor * total).astype(BF)

    outs = [shaped((width, depth) if rows_first else (depth, width), BF)]
    flops = 2 * depth * width * 2 * X * LANES
    return kernel_call(kernel, outs, flops, pos, [rows, blocks])[0]


def exchange(value, axis, groups=None):
    return lax.all_to_all(value, axis, 0, 0, axis_index_groups=groups)


def many(pos, value, count):
    def kernel(pos_ref, value_ref, out_ref, sems):
        copies = [
            pltpu.make_async_copy(value_ref, out_ref.at[index], sems.at[index])
            for index in range(count)
        ]
        for copy in copies:
            copy.start()
        for copy in copies:
            copy.wait()

    outs = [shaped((count,) + value.shape, BF)]
    scratch = [pltpu.SemaphoreType.DMA((count,))]
    return kernel_call(kernel, outs, 0, pos, [value], scratch, (0,), (0,))[0]


def added(pos, value):
    def kernel(pos_ref, value_ref, out_ref):
        total = value_ref[0].astype(F32)
        for index in range(1, value.shape[0]):
            total = total + value_ref[index].astype(F32)
        out_ref[...] = total.astype(BF)

    return kernel_call(kernel, [shaped(value.shape[1:], BF)], value.size, pos, [value])[0]


def in_order(pos, chunks):
    def kernel(pos_ref, *refs):
        for d in range(Z):
            refs[-1][(pos_ref[2] + d) & 3] = refs[d][...]

    return kernel_call(kernel, [shaped((Z,) + chunks[0].shape, BF)], 0, pos, chunks)[0]


def swap_cores(value):
    return lax.ppermute(value, "rep", rep_pairs(0, 0, 1))


def move_x(value, d):
    return lax.ppermute(value, "rep", rep_pairs(d, 0, 0))


def move_z(value, d):
    return lax.ppermute(value, "rep", rep_pairs(0, d, 0))


def total_of(value):
    return jnp.sum(value.astype(F32), axis=0)


def sum_x(keep, sent):
    arrived = lax.optimization_barrier(tuple(move_x(sent[d - 1], d) for d in range(1, X)))
    for part in arrived:
        keep = keep + part.astype(F32)
    return keep.astype(BF)


def scatter_z(value):
    value = value.reshape(Z, value.shape[0] // Z, LANES)
    return exchange(value, "rep", Z_GROUPS)


def spread_z(pos, value):
    whole = in_order(pos, [value] + [move_z(value, -d) for d in range(1, Z)])
    return whole.reshape(Z * value.shape[0], LANES)


def spread_x(value):
    return [value] + [move_x(value, -d) for d in range(1, X)]


def with_other_half(own):
    return own + [swap_cores(part) for part in own]


def body(tokens, first_weight, second_weight, cotangent):
    factor = float(GRP * tokens.shape[0]) ** (-0.5)
    rep = lax.axis_index("rep")
    pos = jnp.stack([rep >> 3, rep & 1, (rep >> 1) & 3]).astype(jnp.int32)

    tok = exchange(many(pos, tokens.T, GRP), "grp")
    first_turned, second_turned, tok = lax.optimization_barrier(
        (first_weight.T, second_weight.T, tok)
    )
    sent = other_half(pos, tok, first_turned)
    keep, sent = own_half(pos, tok, first_turned, swap_cores(sent))
    cot = exchange(many(pos, after(cotangent.T, keep), GRP), "grp")
    value = sum_x(keep, sent)

    sent = other_half(pos, after(cot, value), second_weight)
    keep, sent = own_half(pos, cot, second_weight, swap_cores(sent))

    hidden = total_of(after(scatter_z(value), keep))
    active = jax.nn.gelu(hidden, approximate=False).astype(BF)
    active, hidden = lax.optimization_barrier((active, hidden))
    active = spread_z(pos, active)
    upward = total_of(scatter_z(sum_x(after(keep, active), sent)))
    deltas = (upward * slope(hidden)).astype(BF)

    act = with_other_half(spread_x(active))
    dlt = spread_x(spread_z(pos, deltas))
    out, act = both_halves(pos, act, second_turned)
    out = exchange(out, "grp")
    second_grad = weight_grad(pos, factor, cot, act, False)
    dlt = with_other_half([dlt[0]] + [after(part, second_grad) for part in dlt[1:]])
    back, dlt = both_halves(pos, dlt, first_weight)
    back = exchange(back, "grp")
    first_grad = weight_grad(pos, factor, tok, dlt, True)
    return (added(pos, out).T, added(pos, back).T, first_grad, second_grad)


def solution(mesh):
    in_specs = (P("grp", "rep"), P("rep", "grp"), P("grp", "rep"), P("grp", "rep"))
    out_specs = (P("grp", "rep"), P("grp", "rep"), P("rep", "grp"), P("grp", "rep"))
    return jax.shard_map(body, mesh=mesh, in_specs=in_specs, out_specs=out_specs, check_vma=False)
```

```python
import math

import jax
import jax.numpy as jnp
from jax import lax
from jax.experimental import pallas as pl
from jax.experimental.pallas import tpu as pltpu
from jax.sharding import PartitionSpec as P

BF = jnp.bfloat16
F32 = jnp.float32
GRP = 8
X, Z, C = 4, 4, 2
LANES = 128


def rep_index(x, z, c):
    return (x * Z + z) * C + c


def rep_pairs(dx, dz, dc):
    return [
        (rep_index(x, z, c), rep_index((x + dx) % X, (z + dz) % Z, (c + dc) % C))
        for x in range(X)
        for z in range(Z)
        for c in range(C)
    ]


Z_GROUPS = [[rep_index(x, z, c) for z in range(Z)] for x in range(X) for c in range(C)]


def after(value, *others):
    return lax.optimization_barrier((value,) + others)[0]


def slope(hidden):
    normal_cdf = 0.5 * (1.0 + lax.erf(hidden * (1.0 / math.sqrt(2.0))))
    density = jnp.exp(-0.5 * hidden * hidden) * (1.0 / math.sqrt(2.0 * math.pi))
    return normal_cdf + hidden * density


def dot(left, right, dims):
    return lax.dot_general(left, right, (dims, ((), ())), preferred_element_type=F32)


PLAIN = ((1,), (0,))
LAST = ((1,), (1,))


def shaped(shape, dtype):
    return jax.ShapeDtypeStruct(shape, dtype)


def kernel_call(kernel, outs, flops, pos, operands, scratch=(), far=(), far_in=()):
    moved = sum(math.prod(o.shape) * o.dtype.itemsize for o in [*operands, *outs])
    vmem = pl.BlockSpec(memory_space=pltpu.VMEM)
    hbm = pl.BlockSpec(memory_space=pltpu.HBM)
    return pl.pallas_call(
        kernel,
        out_shape=[pltpu.HBM(o.shape, o.dtype) if i in far else o for i, o in enumerate(outs)],
        in_specs=[pl.BlockSpec(memory_space=pltpu.SMEM)]
        + [hbm if i in far_in else vmem for i in range(len(operands))],
        out_specs=[hbm if i in far else vmem for i in range(len(outs))],
        scratch_shapes=scratch,
        compiler_params=pltpu.CompilerParams(vmem_limit_bytes=16 * 1024 * 1024),
        cost_estimate=pl.CostEstimate(flops=flops, bytes_accessed=moved, transcendentals=0),
    )(pos, *operands)


def half_of(ref, half, x):
    return jnp.concatenate([ref[half * X + ((x + d) & 3)] for d in range(X)], axis=1)


def wide(refs):
    return jnp.concatenate([ref[...] for ref in refs], axis=1)


def block(value, d):
    return value[:, d * LANES : (d + 1) * LANES]


def staged(out):
    return [pltpu.VMEM(out.shape, out.dtype), pltpu.SemaphoreType.DMA(out.shape[:1])]


def other_half(pos, rows, weight):
    depth, width = weight.shape

    def kernel(pos_ref, rows_ref, weight_ref, out_ref, held_ref, sems):
        rows = half_of(rows_ref, 1 - pos_ref[1], pos_ref[0])
        copies = []
        for pair in range(X // 2):
            here = rows[:, pair * 2 * LANES : (pair + 1) * 2 * LANES]
            product = dot(weight_ref[...], here, PLAIN).astype(BF)
            for d in range(2):
                index = pair * 2 + d
                held_ref[index] = block(product, d)
                copies.append(
                    pltpu.make_async_copy(held_ref.at[index], out_ref.at[index], sems.at[index])
                )
                copies[-1].start()
        for copy in copies:
            copy.wait()

    out = shaped((X, depth, LANES), BF)
    flops = 2 * depth * width * X * LANES
    return kernel_call(kernel, [out], flops, pos, [rows, weight], staged(out), (0,))[0]


def own_half(pos, rows, weight, arrived):
    depth, width = weight.shape

    def kernel(pos_ref, rows_ref, weight_ref, arrived_ref, keep_ref, *refs):
        sent, held_ref, sems = refs[: X - 1], refs[-2], refs[-1]
        rows = half_of(rows_ref, pos_ref[1], pos_ref[0])
        copies = []
        for pair in (1, 0):
            here = rows[:, pair * 2 * LANES : (pair + 1) * 2 * LANES]
            product = dot(weight_ref[...], here, PLAIN)
            for i in range(2):
                d = pair * 2 + i
                total = block(product, i) + arrived_ref[d].astype(F32)
                if d == 0:
                    keep_ref[...] = total
                    continue
                held_ref[d - 1] = total.astype(BF)
                copies.append(
                    pltpu.make_async_copy(held_ref.at[d - 1], sent[d - 1], sems.at[d - 1])
                )
                copies[-1].start()
        for copy in copies:
            copy.wait()

    part = shaped((depth, LANES), BF)
    outs = [shaped((depth, LANES), F32)] + [part] * (X - 1)
    scratch = staged(shaped((X - 1,) + part.shape, BF))
    flops = 2 * depth * width * X * LANES
    operands = [rows, weight, arrived]
    keep, *sent = kernel_call(kernel, outs, flops, pos, operands, scratch, range(1, X))
    return keep, sent


def both_halves(pos, blocks, weight):
    depth, width = weight.shape
    count = 2 * X

    def kernel(pos_ref, *refs):
        weight_ref, out_ref, kept_ref, held_ref, out_sems, sems = refs[-6:]
        kept = [
            pltpu.make_async_copy(refs[index], kept_ref.at[index], sems.at[index])
            for index in range(count)
        ]
        for copy in kept:
            copy.start()
        x, c = pos_ref[0], pos_ref[1]
        for part, half in ((refs[:X], c), (refs[X:count], 1 - c)):
            product = dot(weight_ref[...], wide(part), PLAIN).astype(BF)
            for d in range(X):
                index, target = len(kept) - count, half * X + ((x + d) & 3)
                held_ref[index] = block(product, d)
                kept.append(
                    pltpu.make_async_copy(held_ref.at[index], out_ref.at[target], out_sems.at[index])
                )
                kept[-1].start()
        for copy in kept:
            copy.wait()

    outs = [shaped((count, depth, LANES), BF), shaped((count, width, LANES), BF)]
    flops = 2 * depth * width * count * LANES
    scratch = staged(outs[0]) + [pltpu.SemaphoreType.DMA((count,))]
    return kernel_call(kernel, outs, flops, pos, [*blocks, weight], scratch, (0, 1))


def weight_grad(pos, factor, rows, blocks, rows_first):
    width, depth = rows.shape[1], blocks.shape[1]

    def kernel(pos_ref, rows_ref, blocks_ref, out_ref):
        x, c = pos_ref[0], pos_ref[1]
        total = None
        for part, half in ((0, c), (1, 1 - c)):
            pair = half_of(rows_ref, half, x), half_of(blocks_ref, part, 0)
            term = dot(*(pair if rows_first else pair[::-1]), LAST)
            total = term if total is None else total + term
        out_ref[...] = (factor * total).astype(BF)

    outs = [shaped((width, depth) if rows_first else (depth, width), BF)]
    flops = 2 * depth * width * 2 * X * LANES
    return kernel_call(kernel, outs, flops, pos, [rows, blocks])[0]


def exchange(value, axis, groups=None):
    return lax.all_to_all(value, axis, 0, 0, axis_index_groups=groups)


def many(pos, value, count):
    def kernel(pos_ref, value_ref, out_ref, sems):
        copies = [
            pltpu.make_async_copy(value_ref, out_ref.at[index], sems.at[index])
            for index in range(count)
        ]
        for copy in copies:
            copy.start()
        for copy in copies:
            copy.wait()

    outs = [shaped((count,) + value.shape, BF)]
    scratch = [pltpu.SemaphoreType.DMA((count,))]
    return kernel_call(kernel, outs, 0, pos, [value], scratch, (0,), (0,))[0]


def fan_out(value, held_ref, out_ref, sems):
    held_ref[...] = value
    copies = [
        pltpu.make_async_copy(held_ref, out_ref.at[index], sems.at[index]) for index in range(Z)
    ]
    for copy in copies:
        copy.start()
    return copies


def activated(pos, arrived):
    def kernel(pos_ref, arrived_ref, hidden_ref, out_ref, held_ref, sems):
        hidden = total_of(arrived_ref[...])
        cdf = 0.5 * (1.0 + lax.erf(hidden * (1.0 / math.sqrt(2.0))))
        copies = fan_out((hidden * cdf).astype(BF), held_ref, out_ref, sems)
        hidden_ref[...] = hidden
        for copy in copies:
            copy.wait()

    part = arrived.shape[1:]
    outs = [shaped(part, F32), shaped(arrived.shape, BF)]
    scratch = [pltpu.VMEM(part, BF), pltpu.SemaphoreType.DMA((Z,))]
    return kernel_call(kernel, outs, arrived.size, pos, [arrived], scratch, (1,))


def sloped(pos, arrived, hidden):
    def kernel(pos_ref, arrived_ref, hidden_ref, out_ref, held_ref, sems):
        deltas = total_of(arrived_ref[...]) * slope(hidden_ref[...])
        for copy in fan_out(deltas.astype(BF), held_ref, out_ref, sems):
            copy.wait()

    outs = [shaped(arrived.shape, BF)]
    scratch = [pltpu.VMEM(hidden.shape, BF), pltpu.SemaphoreType.DMA((Z,))]
    return kernel_call(kernel, outs, arrived.size, pos, [arrived, hidden], scratch, (0,))[0]


def added(pos, value):
    def kernel(pos_ref, value_ref, out_ref):
        total = value_ref[0].astype(F32)
        for index in range(1, value.shape[0]):
            total = total + value_ref[index].astype(F32)
        out_ref[...] = total.astype(BF)

    return kernel_call(kernel, [shaped(value.shape[1:], BF)], value.size, pos, [value])[0]


def swap_cores(value):
    return lax.ppermute(value, "rep", rep_pairs(0, 0, 1))


def move_x(value, d):
    return lax.ppermute(value, "rep", rep_pairs(d, 0, 0))


def total_of(value):
    return jnp.sum(value.astype(F32), axis=0)


def sum_x(keep, sent):
    arrived = lax.optimization_barrier(tuple(move_x(sent[d - 1], d) for d in range(1, X)))
    for part in arrived:
        keep = keep + part.astype(F32)
    return keep.astype(BF)


def scatter_z(value):
    value = value.reshape(Z, value.shape[0] // Z, LANES)
    return exchange(value, "rep", Z_GROUPS)


def spread_z(value):
    return exchange(value, "rep", Z_GROUPS).reshape(-1, LANES)


def spread_x(value):
    return [value] + [move_x(value, -d) for d in range(1, X)]


def with_other_half(own):
    return own + [swap_cores(part) for part in own]


def body(tokens, first_weight, second_weight, cotangent):
    factor = float(GRP * tokens.shape[0]) ** (-0.5)
    rep = lax.axis_index("rep")
    pos = jnp.stack([rep >> 3, rep & 1, (rep >> 1) & 3]).astype(jnp.int32)

    tok = exchange(many(pos, tokens.T, GRP), "grp")
    first_turned, second_turned, tok = lax.optimization_barrier(
        (first_weight.T, second_weight.T, tok)
    )
    sent = other_half(pos, tok, first_turned)
    keep, sent = own_half(pos, tok, first_turned, swap_cores(sent))
    cot = exchange(many(pos, after(cotangent.T, keep), GRP), "grp")
    value = sum_x(keep, sent)

    sent = other_half(pos, after(cot, value), second_weight)
    keep, sent = own_half(pos, cot, second_weight, swap_cores(sent))

    hidden, active = activated(pos, after(scatter_z(value), keep))
    deltas = sloped(pos, scatter_z(sum_x(keep, sent)), hidden)

    act = with_other_half(spread_x(spread_z(active)))
    dlt = spread_x(spread_z(deltas))
    out, act = both_halves(pos, act, second_turned)
    out = exchange(out, "grp")
    second_grad = weight_grad(pos, factor, cot, act, False)
    dlt = with_other_half([dlt[0]] + [after(part, second_grad) for part in dlt[1:]])
    back, dlt = both_halves(pos, dlt, first_weight)
    back = exchange(back, "grp")
    first_grad = weight_grad(pos, factor, tok, dlt, True)
    return (added(pos, out).T, added(pos, back).T, first_grad, second_grad)


def solution(mesh):
    in_specs = (P("grp", "rep"), P("rep", "grp"), P("grp", "rep"), P("grp", "rep"))
    out_specs = (P("grp", "rep"), P("grp", "rep"), P("rep", "grp"), P("grp", "rep"))
    return jax.shard_map(body, mesh=mesh, in_specs=in_specs, out_specs=out_specs, check_vma=False)
```

```python
import math

import jax
import jax.numpy as jnp
from jax import lax
from jax.experimental import pallas as pl
from jax.experimental.pallas import tpu as pltpu
from jax.sharding import PartitionSpec as P

BF = jnp.bfloat16
F32 = jnp.float32
GRP = 8
X, Z, C = 4, 4, 2
LANES = 128


def rep_index(x, z, c):
    return (x * Z + z) * C + c


def rep_pairs(dx, dz, dc):
    return [
        (rep_index(x, z, c), rep_index((x + dx) % X, (z + dz) % Z, (c + dc) % C))
        for x in range(X)
        for z in range(Z)
        for c in range(C)
    ]


Z_GROUPS = [[rep_index(x, z, c) for z in range(Z)] for x in range(X) for c in range(C)]


def after(value, *others):
    return lax.optimization_barrier((value,) + others)[0]


def slope(hidden):
    normal_cdf = 0.5 * (1.0 + lax.erf(hidden * (1.0 / math.sqrt(2.0))))
    density = jnp.exp(-0.5 * hidden * hidden) * (1.0 / math.sqrt(2.0 * math.pi))
    return normal_cdf + hidden * density


def dot(left, right, dims):
    return lax.dot_general(left, right, (dims, ((), ())), preferred_element_type=F32)


PLAIN = ((1,), (0,))
LAST = ((1,), (1,))


def shaped(shape, dtype):
    return jax.ShapeDtypeStruct(shape, dtype)


def kernel_call(kernel, outs, flops, pos, operands, scratch=(), far=(), far_in=()):
    moved = sum(math.prod(o.shape) * o.dtype.itemsize for o in [*operands, *outs])
    vmem = pl.BlockSpec(memory_space=pltpu.VMEM)
    hbm = pl.BlockSpec(memory_space=pltpu.HBM)
    return pl.pallas_call(
        kernel,
        out_shape=[pltpu.HBM(o.shape, o.dtype) if i in far else o for i, o in enumerate(outs)],
        in_specs=[pl.BlockSpec(memory_space=pltpu.SMEM)]
        + [hbm if i in far_in else vmem for i in range(len(operands))],
        out_specs=[hbm if i in far else vmem for i in range(len(outs))],
        scratch_shapes=scratch,
        compiler_params=pltpu.CompilerParams(vmem_limit_bytes=16 * 1024 * 1024),
        cost_estimate=pl.CostEstimate(flops=flops, bytes_accessed=moved, transcendentals=0),
    )(pos, *operands)


def half_of(ref, half, x):
    return jnp.concatenate([ref[half * X + ((x + d) & 3)] for d in range(X)], axis=1)


def wide(refs):
    return jnp.concatenate([ref[...] for ref in refs], axis=1)


def block(value, d):
    return value[:, d * LANES : (d + 1) * LANES]


def staged(out):
    return [pltpu.VMEM(out.shape, out.dtype), pltpu.SemaphoreType.DMA(out.shape[:1])]


def other_half(pos, rows, weight):
    depth, width = weight.shape

    def kernel(pos_ref, rows_ref, weight_ref, out_ref, held_ref, sems):
        rows = half_of(rows_ref, 1 - pos_ref[1], pos_ref[0])
        copies = []
        for pair in range(X // 2):
            here = rows[:, pair * 2 * LANES : (pair + 1) * 2 * LANES]
            product = dot(weight_ref[...], here, PLAIN).astype(BF)
            for d in range(2):
                index = pair * 2 + d
                held_ref[index] = block(product, d)
                copies.append(
                    pltpu.make_async_copy(held_ref.at[index], out_ref.at[index], sems.at[index])
                )
                copies[-1].start()
        for copy in copies:
            copy.wait()

    out = shaped((X, depth, LANES), BF)
    flops = 2 * depth * width * X * LANES
    return kernel_call(kernel, [out], flops, pos, [rows, weight], staged(out), (0,))[0]


def own_half(pos, rows, weight, arrived):
    depth, width = weight.shape

    def kernel(pos_ref, rows_ref, weight_ref, arrived_ref, keep_ref, *refs):
        sent, held_ref, sems = refs[: X - 1], refs[-2], refs[-1]
        rows = half_of(rows_ref, pos_ref[1], pos_ref[0])
        copies = []
        for pair in (1, 0):
            here = rows[:, pair * 2 * LANES : (pair + 1) * 2 * LANES]
            product = dot(weight_ref[...], here, PLAIN)
            for i in range(2):
                d = pair * 2 + i
                total = block(product, i) + arrived_ref[d].astype(F32)
                if d == 0:
                    keep_ref[...] = total
                    continue
                held_ref[d - 1] = total.astype(BF)
                copies.append(
                    pltpu.make_async_copy(held_ref.at[d - 1], sent[d - 1], sems.at[d - 1])
                )
                copies[-1].start()
        for copy in copies:
            copy.wait()

    part = shaped((depth, LANES), BF)
    outs = [shaped((depth, LANES), F32)] + [part] * (X - 1)
    scratch = staged(shaped((X - 1,) + part.shape, BF))
    flops = 2 * depth * width * X * LANES
    operands = [rows, weight, arrived]
    keep, *sent = kernel_call(kernel, outs, flops, pos, operands, scratch, range(1, X))
    return keep, sent


def both_halves(pos, blocks, weight):
    depth, width = weight.shape
    count = 2 * X

    def kernel(pos_ref, *refs):
        weight_ref, out_ref, kept_ref, held_ref, out_sems, sems = refs[-6:]
        kept = [
            pltpu.make_async_copy(refs[index], kept_ref.at[index], sems.at[index])
            for index in range(count)
        ]
        for copy in kept:
            copy.start()
        x, c = pos_ref[0], pos_ref[1]
        for part, half in ((refs[:X], c), (refs[X:count], 1 - c)):
            product = dot(weight_ref[...], wide(part), PLAIN).astype(BF)
            for d in range(X):
                index, target = len(kept) - count, half * X + ((x + d) & 3)
                held_ref[index] = block(product, d)
                kept.append(
                    pltpu.make_async_copy(held_ref.at[index], out_ref.at[target], out_sems.at[index])
                )
                kept[-1].start()
        for copy in kept:
            copy.wait()

    outs = [shaped((count, depth, LANES), BF), shaped((count, width, LANES), BF)]
    flops = 2 * depth * width * count * LANES
    scratch = staged(outs[0]) + [pltpu.SemaphoreType.DMA((count,))]
    return kernel_call(kernel, outs, flops, pos, [*blocks, weight], scratch, (0, 1))


def weight_grad(pos, factor, rows, blocks, rows_first):
    width, depth = rows.shape[1], blocks.shape[1]

    def kernel(pos_ref, rows_ref, blocks_ref, out_ref):
        x, c = pos_ref[0], pos_ref[1]
        total = None
        for part, half in ((0, c), (1, 1 - c)):
            pair = half_of(rows_ref, half, x), half_of(blocks_ref, part, 0)
            term = dot(*(pair if rows_first else pair[::-1]), LAST)
            total = term if total is None else total + term
        out_ref[...] = (factor * total).astype(BF)

    outs = [shaped((width, depth) if rows_first else (depth, width), BF)]
    flops = 2 * depth * width * 2 * X * LANES
    return kernel_call(kernel, outs, flops, pos, [rows, blocks])[0]


def exchange(value, axis, groups=None):
    return lax.all_to_all(value, axis, 0, 0, axis_index_groups=groups)


def many(pos, value, count):
    def kernel(pos_ref, value_ref, out_ref, sems):
        copies = [
            pltpu.make_async_copy(value_ref, out_ref.at[index], sems.at[index])
            for index in range(count)
        ]
        for copy in copies:
            copy.start()
        for copy in copies:
            copy.wait()

    outs = [shaped((count,) + value.shape, BF)]
    scratch = [pltpu.SemaphoreType.DMA((count,))]
    value = pltpu.with_memory_space_constraint(value, pltpu.HBM)
    return kernel_call(kernel, outs, 0, pos, [value], scratch, (0,), (0,))[0]


def fan_out(value, held_ref, out_ref, sems):
    held_ref[...] = value
    copies = [
        pltpu.make_async_copy(held_ref, out_ref.at[index], sems.at[index]) for index in range(Z)
    ]
    for copy in copies:
        copy.start()
    return copies


def activated(pos, arrived):
    def kernel(pos_ref, arrived_ref, hidden_ref, out_ref, held_ref, sems):
        hidden = total_of(arrived_ref[...])
        cdf = 0.5 * (1.0 + lax.erf(hidden * (1.0 / math.sqrt(2.0))))
        copies = fan_out((hidden * cdf).astype(BF), held_ref, out_ref, sems)
        hidden_ref[...] = hidden
        for copy in copies:
            copy.wait()

    part = arrived.shape[1:]
    outs = [shaped(part, F32), shaped(arrived.shape, BF)]
    scratch = [pltpu.VMEM(part, BF), pltpu.SemaphoreType.DMA((Z,))]
    return kernel_call(kernel, outs, arrived.size, pos, [arrived], scratch, (1,))


def sloped(pos, arrived, hidden):
    def kernel(pos_ref, arrived_ref, hidden_ref, out_ref, held_ref, sems):
        deltas = total_of(arrived_ref[...]) * slope(hidden_ref[...])
        for copy in fan_out(deltas.astype(BF), held_ref, out_ref, sems):
            copy.wait()

    outs = [shaped(arrived.shape, BF)]
    scratch = [pltpu.VMEM(hidden.shape, BF), pltpu.SemaphoreType.DMA((Z,))]
    return kernel_call(kernel, outs, arrived.size, pos, [arrived, hidden], scratch, (0,))[0]


def added(pos, value):
    def kernel(pos_ref, value_ref, out_ref):
        total = value_ref[0].astype(F32)
        for index in range(1, value.shape[0]):
            total = total + value_ref[index].astype(F32)
        out_ref[...] = total.astype(BF)

    return kernel_call(kernel, [shaped(value.shape[1:], BF)], value.size, pos, [value])[0]


def swap_cores(value):
    return lax.ppermute(value, "rep", rep_pairs(0, 0, 1))


def move_x(value, d):
    return lax.ppermute(value, "rep", rep_pairs(d, 0, 0))


def total_of(value):
    return jnp.sum(value.astype(F32), axis=0)


def sum_x(keep, sent):
    arrived = lax.optimization_barrier(tuple(move_x(sent[d - 1], d) for d in range(1, X)))
    for part in arrived:
        keep = keep + part.astype(F32)
    return keep.astype(BF)


def scatter_z(value):
    value = value.reshape(Z, value.shape[0] // Z, LANES)
    return exchange(value, "rep", Z_GROUPS)


def spread_z(value):
    return exchange(value, "rep", Z_GROUPS).reshape(-1, LANES)


def spread_x(value):
    return [value] + [move_x(value, -d) for d in range(1, X)]


def with_other_half(own):
    return own + [swap_cores(part) for part in own]


def body(tokens, first_weight, second_weight, cotangent):
    factor = float(GRP * tokens.shape[0]) ** (-0.5)
    rep = lax.axis_index("rep")
    pos = jnp.stack([rep >> 3, rep & 1, (rep >> 1) & 3]).astype(jnp.int32)

    tok = exchange(many(pos, tokens.T, GRP), "grp")
    first_turned, second_turned, cots, tok = lax.optimization_barrier(
        (first_weight.T, second_weight.T, many(pos, cotangent.T, GRP), tok)
    )
    sent = other_half(pos, tok, first_turned)
    keep, sent = own_half(pos, tok, first_turned, swap_cores(sent))
    cot = exchange(after(cots, keep), "grp")
    value = sum_x(keep, sent)

    sent = other_half(pos, after(cot, value), second_weight)
    keep, sent = own_half(pos, cot, second_weight, swap_cores(sent))

    hidden, active = activated(pos, after(scatter_z(value), keep))
    deltas = sloped(pos, scatter_z(sum_x(keep, sent)), hidden)

    act = with_other_half(spread_x(spread_z(active)))
    dlt = spread_x(spread_z(deltas))
    out, act = both_halves(pos, act, second_turned)
    out = exchange(out, "grp")
    second_grad = weight_grad(pos, factor, cot, act, False)
    dlt = with_other_half([dlt[0]] + [after(part, second_grad) for part in dlt[1:]])
    back, dlt = both_halves(pos, dlt, first_weight)
    back = exchange(back, "grp")
    first_grad = weight_grad(pos, factor, tok, dlt, True)
    return (added(pos, out).T, added(pos, back).T, first_grad, second_grad)


def solution(mesh):
    in_specs = (P("grp", "rep"), P("rep", "grp"), P("grp", "rep"), P("grp", "rep"))
    out_specs = (P("grp", "rep"), P("grp", "rep"), P("rep", "grp"), P("grp", "rep"))
    return jax.shard_map(body, mesh=mesh, in_specs=in_specs, out_specs=out_specs, check_vma=False)
```

```python
import math

import jax
import jax.numpy as jnp
from jax import lax
from jax.experimental import pallas as pl
from jax.experimental.pallas import tpu as pltpu
from jax.sharding import PartitionSpec as P

BF = jnp.bfloat16
F32 = jnp.float32
GRP = 8
X, Z, C = 4, 4, 2
LANES = 128
PIECES = 2


def rep_index(x, z, c):
    return (x * Z + z) * C + c


def rep_pairs(dx, dz, dc):
    return [
        (rep_index(x, z, c), rep_index((x + dx) % X, (z + dz) % Z, (c + dc) % C))
        for x in range(X)
        for z in range(Z)
        for c in range(C)
    ]


Z_GROUPS = [[rep_index(x, z, c) for z in range(Z)] for x in range(X) for c in range(C)]


def after(value, *others):
    return lax.optimization_barrier((value,) + others)[0]


def slope(hidden):
    normal_cdf = 0.5 * (1.0 + lax.erf(hidden * (1.0 / math.sqrt(2.0))))
    density = jnp.exp(-0.5 * hidden * hidden) * (1.0 / math.sqrt(2.0 * math.pi))
    return normal_cdf + hidden * density


def dot(left, right, dims):
    return lax.dot_general(left, right, (dims, ((), ())), preferred_element_type=F32)


PLAIN = ((1,), (0,))
LAST = ((1,), (1,))


def shaped(shape, dtype):
    return jax.ShapeDtypeStruct(shape, dtype)


def kernel_call(kernel, outs, flops, pos, operands, scratch=(), far=(), far_in=()):
    moved = sum(math.prod(o.shape) * o.dtype.itemsize for o in [*operands, *outs])
    vmem = pl.BlockSpec(memory_space=pltpu.VMEM)
    hbm = pl.BlockSpec(memory_space=pltpu.HBM)
    return pl.pallas_call(
        kernel,
        out_shape=[pltpu.HBM(o.shape, o.dtype) if i in far else o for i, o in enumerate(outs)],
        in_specs=[pl.BlockSpec(memory_space=pltpu.SMEM)]
        + [hbm if i in far_in else vmem for i in range(len(operands))],
        out_specs=[hbm if i in far else vmem for i in range(len(outs))],
        scratch_shapes=scratch,
        compiler_params=pltpu.CompilerParams(vmem_limit_bytes=16 * 1024 * 1024),
        cost_estimate=pl.CostEstimate(flops=flops, bytes_accessed=moved, transcendentals=0),
    )(pos, *operands)


def half_of(ref, half, x):
    return jnp.concatenate([ref[half * X + ((x + d) & 3)] for d in range(X)], axis=1)


def wide(refs):
    return jnp.concatenate([ref[...] for ref in refs], axis=1)


def block(value, d):
    return value[:, d * LANES : (d + 1) * LANES]


def staged(out):
    return [pltpu.VMEM(out.shape, out.dtype), pltpu.SemaphoreType.DMA(out.shape[:1])]


def other_half(pos, rows, weight):
    depth, width = weight.shape
    each = X // PIECES

    def kernel(pos_ref, rows_ref, weight_ref, *refs):
        outs, held_ref, sems = refs[:PIECES], refs[-2], refs[-1]
        rows = half_of(rows_ref, 1 - pos_ref[1], pos_ref[0])
        copies = []
        for pair in range(X // 2):
            here = rows[:, pair * 2 * LANES : (pair + 1) * 2 * LANES]
            product = dot(weight_ref[...], here, PLAIN).astype(BF)
            for d in range(2):
                index = pair * 2 + d
                held_ref[index] = block(product, d)
                target = outs[index // each].at[index % each]
                copies.append(pltpu.make_async_copy(held_ref.at[index], target, sems.at[index]))
                copies[-1].start()
        for copy in copies:
            copy.wait()

    outs = [shaped((each, depth, LANES), BF)] * PIECES
    flops = 2 * depth * width * X * LANES
    scratch = staged(shaped((X, depth, LANES), BF))
    return kernel_call(kernel, outs, flops, pos, [rows, weight], scratch, range(PIECES))


def own_half(pos, rows, weight, arrived):
    depth, width = weight.shape

    def kernel(pos_ref, rows_ref, weight_ref, *refs):
        arrived, keep_ref = refs[:PIECES], refs[PIECES]
        sent, held_ref, sems = refs[PIECES + 1 : -2], refs[-2], refs[-1]
        rows = half_of(rows_ref, pos_ref[1], pos_ref[0])
        copies = []
        for pair in (1, 0):
            here = rows[:, pair * 2 * LANES : (pair + 1) * 2 * LANES]
            product = dot(weight_ref[...], here, PLAIN)
            for i in range(2):
                d = pair * 2 + i
                other = arrived[d * PIECES // X][d % (X // PIECES)]
                total = block(product, i) + other.astype(F32)
                if d == 0:
                    keep_ref[...] = total
                    continue
                held_ref[d - 1] = total.astype(BF)
                copies.append(
                    pltpu.make_async_copy(held_ref.at[d - 1], sent[d - 1], sems.at[d - 1])
                )
                copies[-1].start()
        for copy in copies:
            copy.wait()

    part = shaped((depth, LANES), BF)
    outs = [shaped((depth, LANES), F32)] + [part] * (X - 1)
    scratch = staged(shaped((X - 1,) + part.shape, BF))
    flops = 2 * depth * width * X * LANES
    operands = [rows, weight, *arrived]
    keep, *sent = kernel_call(kernel, outs, flops, pos, operands, scratch, range(1, X))
    return keep, sent


def both_halves(pos, blocks, weight):
    depth, width = weight.shape
    count = 2 * X

    def kernel(pos_ref, *refs):
        weight_ref, out_ref, kept_ref, held_ref, out_sems, sems = refs[-6:]
        kept = [
            pltpu.make_async_copy(refs[index], kept_ref.at[index], sems.at[index])
            for index in range(count)
        ]
        for copy in kept:
            copy.start()
        x, c = pos_ref[0], pos_ref[1]
        for part, half in ((refs[:X], c), (refs[X:count], 1 - c)):
            product = dot(weight_ref[...], wide(part), PLAIN).astype(BF)
            for d in range(X):
                index, target = len(kept) - count, half * X + ((x + d) & 3)
                held_ref[index] = block(product, d)
                kept.append(
                    pltpu.make_async_copy(held_ref.at[index], out_ref.at[target], out_sems.at[index])
                )
                kept[-1].start()
        for copy in kept:
            copy.wait()

    outs = [shaped((count, depth, LANES), BF), shaped((count, width, LANES), BF)]
    flops = 2 * depth * width * count * LANES
    scratch = staged(outs[0]) + [pltpu.SemaphoreType.DMA((count,))]
    return kernel_call(kernel, outs, flops, pos, [*blocks, weight], scratch, (0, 1))


def weight_grad(pos, factor, rows, blocks, rows_first):
    width, depth = rows.shape[1], blocks.shape[1]

    def kernel(pos_ref, rows_ref, blocks_ref, out_ref):
        x, c = pos_ref[0], pos_ref[1]
        total = None
        for part, half in ((0, c), (1, 1 - c)):
            pair = half_of(rows_ref, half, x), half_of(blocks_ref, part, 0)
            term = dot(*(pair if rows_first else pair[::-1]), LAST)
            total = term if total is None else total + term
        out_ref[...] = (factor * total).astype(BF)

    outs = [shaped((width, depth) if rows_first else (depth, width), BF)]
    flops = 2 * depth * width * 2 * X * LANES
    return kernel_call(kernel, outs, flops, pos, [rows, blocks])[0]


def exchange(value, axis, groups=None):
    return lax.all_to_all(value, axis, 0, 0, axis_index_groups=groups)


def many(pos, value, count):
    def kernel(pos_ref, value_ref, out_ref, sems):
        copies = [
            pltpu.make_async_copy(value_ref, out_ref.at[index], sems.at[index])
            for index in range(count)
        ]
        for copy in copies:
            copy.start()
        for copy in copies:
            copy.wait()

    outs = [shaped((count,) + value.shape, BF)]
    scratch = [pltpu.SemaphoreType.DMA((count,))]
    return kernel_call(kernel, outs, 0, pos, [value], scratch, (0,))[0]


def fan_out(value, held_ref, out_ref, sems):
    held_ref[...] = value
    copies = [
        pltpu.make_async_copy(held_ref, out_ref.at[index], sems.at[index]) for index in range(Z)
    ]
    for copy in copies:
        copy.start()
    return copies


def activated(pos, arrived):
    def kernel(pos_ref, arrived_ref, hidden_ref, out_ref, held_ref, sems):
        hidden = total_of(arrived_ref[...])
        cdf = 0.5 * (1.0 + lax.erf(hidden * (1.0 / math.sqrt(2.0))))
        copies = fan_out((hidden * cdf).astype(BF), held_ref, out_ref, sems)
        hidden_ref[...] = hidden
        for copy in copies:
            copy.wait()

    part = arrived.shape[1:]
    outs = [shaped(part, F32), shaped(arrived.shape, BF)]
    scratch = [pltpu.VMEM(part, BF), pltpu.SemaphoreType.DMA((Z,))]
    return kernel_call(kernel, outs, arrived.size, pos, [arrived], scratch, (1,))


def sloped(pos, arrived, hidden):
    def kernel(pos_ref, arrived_ref, hidden_ref, out_ref, held_ref, sems):
        deltas = total_of(arrived_ref[...]) * slope(hidden_ref[...])
        for copy in fan_out(deltas.astype(BF), held_ref, out_ref, sems):
            copy.wait()

    outs = [shaped(arrived.shape, BF)]
    scratch = [pltpu.VMEM(hidden.shape, BF), pltpu.SemaphoreType.DMA((Z,))]
    return kernel_call(kernel, outs, arrived.size, pos, [arrived, hidden], scratch, (0,))[0]


def added(pos, value):
    def kernel(pos_ref, value_ref, out_ref):
        total = value_ref[0].astype(F32)
        for index in range(1, value.shape[0]):
            total = total + value_ref[index].astype(F32)
        out_ref[...] = total.astype(BF)

    return kernel_call(kernel, [shaped(value.shape[1:], BF)], value.size, pos, [value])[0]


def swap_cores(value):
    return lax.ppermute(value, "rep", rep_pairs(0, 0, 1))


def move_x(value, d):
    return lax.ppermute(value, "rep", rep_pairs(d, 0, 0))


def total_of(value):
    return jnp.sum(value.astype(F32), axis=0)


def sum_x(keep, sent):
    arrived = lax.optimization_barrier(tuple(move_x(sent[d - 1], d) for d in range(1, X)))
    for part in arrived:
        keep = keep + part.astype(F32)
    return keep.astype(BF)


def scatter_z(value):
    value = value.reshape(Z, value.shape[0] // Z, LANES)
    return exchange(value, "rep", Z_GROUPS)


def spread_z(value):
    return exchange(value, "rep", Z_GROUPS).reshape(-1, LANES)


def spread_x(value):
    return [value] + [move_x(value, -d) for d in range(1, X)]


def with_other_half(own):
    return own + [swap_cores(part) for part in own]


def body(tokens, first_weight, second_weight, cotangent):
    factor = float(GRP * tokens.shape[0]) ** (-0.5)
    rep = lax.axis_index("rep")
    pos = jnp.stack([rep >> 3, rep & 1, (rep >> 1) & 3]).astype(jnp.int32)

    tok = exchange(many(pos, tokens.T, GRP), "grp")
    first_turned, second_turned, cots, tok = lax.optimization_barrier(
        (first_weight.T, second_weight.T, many(pos, cotangent.T, GRP), tok)
    )
    sent = other_half(pos, tok, first_turned)
    keep, sent = own_half(pos, tok, first_turned, [swap_cores(part) for part in sent])
    cot = exchange(after(cots, keep), "grp")
    value = sum_x(keep, sent)

    sent = other_half(pos, after(cot, keep), second_weight)
    keep, sent = own_half(pos, cot, second_weight, [swap_cores(part) for part in sent])

    hidden, active = activated(pos, after(scatter_z(value), keep))
    deltas = sloped(pos, scatter_z(sum_x(keep, sent)), hidden)

    act = with_other_half(spread_x(spread_z(active)))
    dlt = spread_x(spread_z(deltas))
    out, act = both_halves(pos, act, second_turned)
    out = exchange(out, "grp")
    second_grad = weight_grad(pos, factor, cot, act, False)
    dlt = with_other_half([dlt[0]] + [after(part, second_grad) for part in dlt[1:]])
    back, dlt = both_halves(pos, dlt, first_weight)
    back = exchange(back, "grp")
    first_grad = weight_grad(pos, factor, tok, dlt, True)
    return (added(pos, out).T, added(pos, back).T, first_grad, second_grad)


def solution(mesh):
    in_specs = (P("grp", "rep"), P("rep", "grp"), P("grp", "rep"), P("grp", "rep"))
    out_specs = (P("grp", "rep"), P("grp", "rep"), P("rep", "grp"), P("grp", "rep"))
    return jax.shard_map(body, mesh=mesh, in_specs=in_specs, out_specs=out_specs, check_vma=False)
```

```python
import math

import jax
import jax.numpy as jnp
from jax import lax
from jax.experimental import pallas as pl
from jax.experimental.pallas import tpu as pltpu
from jax.sharding import PartitionSpec as P

BF = jnp.bfloat16
F32 = jnp.float32
GRP = 8
X, Z, C = 4, 4, 2
LANES = 128
TILE = 16


def rep_index(x, z, c):
    return (x * Z + z) * C + c


XZ_GROUPS = [[rep_index(x, z, c) for x in range(X) for z in range(Z)] for c in range(C)]
CORE_PAIRS = [
    (rep_index(x, z, c), rep_index(x, z, 1 - c))
    for x in range(X)
    for z in range(Z)
    for c in range(C)
]
PLAIN = ((1,), (0,))
LAST = ((1,), (1,))


def slope(hidden):
    normal_cdf = 0.5 * (1.0 + lax.erf(hidden * (1.0 / math.sqrt(2.0))))
    density = jnp.exp(-0.5 * hidden * hidden) * (1.0 / math.sqrt(2.0 * math.pi))
    return normal_cdf + hidden * density


def dot(left, right, dims):
    return lax.dot_general(left, right, (dims, ((), ())), preferred_element_type=F32)


def shaped(shape, dtype=BF):
    return jax.ShapeDtypeStruct(shape, dtype)


def room(shape, *copies):
    return [pltpu.VMEM(shape, BF), pltpu.SemaphoreType.DMA(copies)]


def kernel_call(kernel, outs, flops, core, operands, scratch=(), far=(), alias=None):
    moved = sum(math.prod(o.shape) * o.dtype.itemsize for o in [*operands, *outs])
    vmem = pl.BlockSpec(memory_space=pltpu.VMEM)
    hbm = pl.BlockSpec(memory_space=pltpu.HBM)
    return pl.pallas_call(
        kernel,
        out_shape=[pltpu.HBM(o.shape, o.dtype) if i in far else o for i, o in enumerate(outs)],
        in_specs=[pl.BlockSpec(memory_space=pltpu.SMEM)]
        + [hbm if i == alias else vmem for i in range(len(operands))],
        out_specs=[hbm if i in far else vmem for i in range(len(outs))],
        scratch_shapes=scratch,
        input_output_aliases={} if alias is None else {alias + 1: 0},
        compiler_params=pltpu.CompilerParams(vmem_limit_bytes=24 * 1024 * 1024),
        cost_estimate=pl.CostEstimate(flops=flops, bytes_accessed=moved, transcendentals=0),
    )(core, *operands)


def start(copies, source, target, sem):
    copies.append(pltpu.make_async_copy(source, target, sem))
    copies[-1].start()


def finish(copies):
    for copy in copies:
        copy.wait()


def half_of(ref, half, here):
    return jnp.concatenate([ref[half * X + k, here] for k in range(X)], axis=1)


def block(value, k):
    return value[:, k * LANES : (k + 1) * LANES]


def many(core, first, second):
    rows = first.shape[0]

    def kernel(core_ref, first_ref, second_ref, out_ref, sems):
        copies = []
        for index in range(GRP):
            for part, ref in enumerate((first_ref, second_ref)):
                target = out_ref.at[index, pl.ds(part * rows, rows)]
                start(copies, ref, target, sems.at[index, part])
        finish(copies)

    outs = [shaped((GRP, 2 * rows, LANES))]
    scratch = [pltpu.SemaphoreType.DMA((GRP, 2))]
    return kernel_call(kernel, outs, 0, core, [first, second], scratch, (0,))[0]


def other_half(core, rows, here, weight):
    depth, width = weight.shape

    def kernel(core_ref, rows_ref, weight_ref, out_ref, held_ref, sems):
        rows = half_of(rows_ref, 1 - core_ref[0], here)
        copies = []
        for pair in range(X // 2):
            two = rows[:, pair * 2 * LANES : (pair + 1) * 2 * LANES]
            product = dot(weight_ref[...], two, PLAIN).astype(BF)
            for i in range(2):
                k = pair * 2 + i
                held_ref[k] = block(product, i)
                start(copies, held_ref.at[k], out_ref.at[k], sems.at[k])
        finish(copies)

    shape = (X, depth, LANES)
    flops = 2 * depth * width * X * LANES
    return kernel_call(kernel, [shaped(shape)], flops, core, [rows, weight], room(shape, X), (0,))[0]


def own_half(core, rows, here, weight, arrived, part, chunk, before=None):
    depth, width = weight.shape

    def kernel(core_ref, rows_ref, weight_ref, arrived_ref, *refs):
        out_ref, held_ref, sems = refs[-3:]
        rows = half_of(rows_ref, core_ref[0], here)
        copies = []
        for pair in range(X // 2):
            two = rows[:, pair * 2 * LANES : (pair + 1) * 2 * LANES]
            product = dot(weight_ref[...], two, PLAIN)
            for i in range(2):
                k = pair * 2 + i
                total = block(product, i) + arrived_ref[k].astype(F32)
                for z in range(Z):
                    index, lower = k * Z + z, z * chunk
                    count = min(chunk, depth - lower)
                    held_ref[index, :count] = total[lower : lower + count].astype(BF)
                    if count < chunk:
                        held_ref[index, count:] = jnp.zeros((chunk - count, LANES), BF)
                    start(copies, held_ref.at[index], out_ref.at[index, part], sems.at[index])
        finish(copies)

    outs = [shaped((X * Z, 2, chunk, LANES))]
    flops = 2 * depth * width * X * LANES
    operands = [rows, weight, arrived] + ([] if before is None else [before])
    scratch = room((X * Z, chunk, LANES), X * Z)
    alias = None if before is None else 3
    return kernel_call(kernel, outs, flops, core, operands, scratch, (0,), alias)[0]


def middle(core, arrived):
    count, _, chunk, _ = arrived.shape

    def kernel(core_ref, arrived_ref, out_ref, held_ref, sems):
        hidden, upward = arrived_ref[0, 0].astype(F32), arrived_ref[0, 1].astype(F32)
        for index in range(1, count):
            hidden = hidden + arrived_ref[index, 0].astype(F32)
            upward = upward + arrived_ref[index, 1].astype(F32)
        cdf = 0.5 * (1.0 + lax.erf(hidden * (1.0 / math.sqrt(2.0))))
        held_ref[0] = (hidden * cdf).astype(BF)
        held_ref[1] = (upward * slope(hidden)).astype(BF)
        copies = []
        for index in range(count):
            start(copies, held_ref, out_ref.at[index], sems.at[index])
        finish(copies)

    outs = [shaped(arrived.shape)]
    scratch = room(arrived.shape[1:], count)
    return kernel_call(kernel, outs, arrived.size, core, [arrived], scratch, (0,))[0]


def gathered(ref, part, wide_ref):
    depth, chunk = wide_ref.shape[0], ref.shape[2]
    for k in range(X):
        for z in range(Z):
            lower = z * chunk
            count = min(chunk, depth - lower)
            wide_ref[lower : lower + count, k * LANES : (k + 1) * LANES] = ref[k * Z + z, part, :count]
    return wide_ref[...]


def back_products(core, chunks, own, weights, before=None):
    width, depth = weights[0].shape

    def kernel(core_ref, chunks_ref, first_ref, second_ref, *refs):
        out_ref, kept_ref, wide_ref, held_ref, sems, kept_sem = refs[-6:]
        copies = []
        start(copies, chunks_ref, kept_ref, kept_sem)
        half = core_ref[0] if own else 1 - core_ref[0]
        for part, weight_ref in enumerate((first_ref, second_ref)):
            product = dot(weight_ref[...], gathered(chunks_ref, part, wide_ref), PLAIN).astype(BF)
            for k in range(X):
                held_ref[part, k] = block(product, k)
                target = out_ref.at[half * X + k, pl.ds(part * width, width)]
                start(copies, held_ref.at[part, k], target, sems.at[part, k])
        finish(copies)

    outs = [shaped((GRP, 2 * width, LANES)), shaped(chunks.shape)]
    flops = 4 * depth * width * X * LANES
    scratch = [pltpu.VMEM((depth, X * LANES), BF)] + room((2, X, width, LANES), 2, X)
    scratch += [pltpu.SemaphoreType.DMA]
    operands = [chunks, *weights] + ([] if before is None else [before])
    alias = None if before is None else 3
    return kernel_call(kernel, outs, flops, core, operands, scratch, (0, 1), alias)


def weight_grad(core, factor, rows, here, own, other, part, depth, rows_first):
    width = here.stop - here.start

    def kernel(core_ref, rows_ref, own_ref, other_ref, out_ref, wide_ref):
        total = None
        for ref, half in ((own_ref, core_ref[0]), (other_ref, 1 - core_ref[0])):
            pair = half_of(rows_ref, half, here), gathered(ref, part, wide_ref)
            term = dot(*(pair if rows_first else pair[::-1]), LAST)
            total = term if total is None else total + term
        out_ref[...] = (factor * total).astype(BF)

    outs = [shaped((width, depth) if rows_first else (depth, width))]
    flops = 4 * depth * width * X * LANES
    scratch = [pltpu.VMEM((depth, X * LANES), BF)]
    return kernel_call(kernel, outs, flops, core, [rows, own, other], scratch)[0]


def added(core, value):
    rows = value.shape[1] // 2

    def kernel(core_ref, value_ref, *outs):
        for part, out_ref in enumerate(outs):
            here = slice(part * rows, (part + 1) * rows)
            total = value_ref[0, here].astype(F32)
            for index in range(1, value.shape[0]):
                total = total + value_ref[index, here].astype(F32)
            out_ref[...] = total.astype(BF)

    return kernel_call(kernel, [shaped((rows, LANES))] * 2, value.size, core, [value])


def over_grp(value):
    return lax.all_to_all(value, "grp", 0, 0)


def over_xz(value):
    return lax.all_to_all(value, "rep", 0, 0, axis_index_groups=XZ_GROUPS)


def swap_cores(value):
    return lax.ppermute(value, "rep", CORE_PAIRS)


def body(tokens, first_weight, second_weight, cotangent):
    factor = float(GRP * tokens.shape[0]) ** (-0.5)
    width, depth = first_weight.shape
    chunk = -(-depth // (Z * TILE)) * TILE
    core = (lax.axis_index("rep") & 1).astype(jnp.int32).reshape(1)
    tok, cot = slice(0, width), slice(width, 2 * width)

    rows = over_grp(many(core, tokens.T, cotangent.T))
    first_turned, second_turned, rows = lax.optimization_barrier(
        (first_weight.T, second_weight.T, rows)
    )
    sent = other_half(core, rows, tok, first_turned), other_half(core, rows, cot, second_weight)
    sent = [swap_cores(part) for part in sent]
    sums = own_half(core, rows, tok, first_turned, sent[0], 0, chunk)
    sums = own_half(core, rows, cot, second_weight, sent[1], 1, chunk, sums)

    own = over_xz(middle(core, over_xz(sums)))
    other = swap_cores(own)
    weights = [second_turned, first_weight]
    outs, own = back_products(core, own, True, weights)
    outs, other = back_products(core, other, False, weights, outs)
    out, back = added(core, over_grp(outs))
    first_grad = weight_grad(core, factor, rows, tok, own, other, 1, depth, True)
    second_grad = weight_grad(core, factor, rows, cot, own, other, 0, depth, False)
    return (out.T, back.T, first_grad, second_grad)


def solution(mesh):
    in_specs = (P("grp", "rep"), P("rep", "grp"), P("grp", "rep"), P("grp", "rep"))
    out_specs = (P("grp", "rep"), P("grp", "rep"), P("rep", "grp"), P("grp", "rep"))
    return jax.shard_map(body, mesh=mesh, in_specs=in_specs, out_specs=out_specs, check_vma=False)
```

```python
import math

import jax
import jax.numpy as jnp
from jax import lax
from jax.experimental import pallas as pl
from jax.experimental.pallas import tpu as pltpu
from jax.sharding import PartitionSpec as P

BF = jnp.bfloat16
F32 = jnp.float32
GRP = 8
X, Z, C = 4, 4, 2
LANES = 128
PIECES = 2


def rep_index(x, z, c):
    return (x * Z + z) * C + c


def rep_pairs(dx, dz, dc):
    return [
        (rep_index(x, z, c), rep_index((x + dx) % X, (z + dz) % Z, (c + dc) % C))
        for x in range(X)
        for z in range(Z)
        for c in range(C)
    ]


Z_GROUPS = [[rep_index(x, z, c) for z in range(Z)] for x in range(X) for c in range(C)]


def after(value, *others):
    return lax.optimization_barrier((value,) + others)[0]


def slope(hidden):
    normal_cdf = 0.5 * (1.0 + lax.erf(hidden * (1.0 / math.sqrt(2.0))))
    density = jnp.exp(-0.5 * hidden * hidden) * (1.0 / math.sqrt(2.0 * math.pi))
    return normal_cdf + hidden * density


def dot(left, right, dims):
    return lax.dot_general(left, right, (dims, ((), ())), preferred_element_type=F32)


PLAIN = ((1,), (0,))
LAST = ((1,), (1,))


def shaped(shape, dtype):
    return jax.ShapeDtypeStruct(shape, dtype)


def kernel_call(kernel, outs, flops, pos, operands, scratch=(), far=(), far_in=()):
    moved = sum(math.prod(o.shape) * o.dtype.itemsize for o in [*operands, *outs])
    vmem = pl.BlockSpec(memory_space=pltpu.VMEM)
    hbm = pl.BlockSpec(memory_space=pltpu.HBM)
    anywhere = pl.BlockSpec(memory_space=pl.ANY)
    return pl.pallas_call(
        kernel,
        out_shape=[pltpu.HBM(o.shape, o.dtype) if i in far else o for i, o in enumerate(outs)],
        in_specs=[pl.BlockSpec(memory_space=pltpu.SMEM)]
        + [anywhere if i in far_in else vmem for i in range(len(operands))],
        out_specs=[hbm if i in far else vmem for i in range(len(outs))],
        scratch_shapes=scratch,
        compiler_params=pltpu.CompilerParams(vmem_limit_bytes=16 * 1024 * 1024),
        cost_estimate=pl.CostEstimate(flops=flops, bytes_accessed=moved, transcendentals=0),
    )(pos, *operands)


def half_of(ref, half, x):
    return jnp.concatenate([ref[half * X + ((x + d) & 3)] for d in range(X)], axis=1)


def block(value, d):
    return value[:, d * LANES : (d + 1) * LANES]


def staged(out):
    return [pltpu.VMEM(out.shape, out.dtype), pltpu.SemaphoreType.DMA(out.shape[:1])]


def other_half(pos, rows, weight):
    depth, width = weight.shape
    each = X // PIECES

    def kernel(pos_ref, rows_ref, weight_ref, *refs):
        outs, held_ref, sems = refs[:PIECES], refs[-2], refs[-1]
        rows = half_of(rows_ref, 1 - pos_ref[1], pos_ref[0])
        copies = []
        for pair in range(X // 2):
            here = rows[:, pair * 2 * LANES : (pair + 1) * 2 * LANES]
            product = dot(weight_ref[...], here, PLAIN).astype(BF)
            for d in range(2):
                index = pair * 2 + d
                held_ref[index] = block(product, d)
                target = outs[index // each].at[index % each]
                copies.append(pltpu.make_async_copy(held_ref.at[index], target, sems.at[index]))
                copies[-1].start()
        for copy in copies:
            copy.wait()

    outs = [shaped((each, depth, LANES), BF)] * PIECES
    flops = 2 * depth * width * X * LANES
    scratch = staged(shaped((X, depth, LANES), BF))
    return kernel_call(kernel, outs, flops, pos, [rows, weight], scratch, range(PIECES))


def own_half(pos, rows, weight, arrived):
    depth, width = weight.shape

    def kernel(pos_ref, rows_ref, weight_ref, *refs):
        arrived, keep_ref = refs[:PIECES], refs[PIECES]
        sent, held_ref, sems = refs[PIECES + 1 : -2], refs[-2], refs[-1]
        rows = half_of(rows_ref, pos_ref[1], pos_ref[0])
        copies = []
        for pair in (1, 0):
            here = rows[:, pair * 2 * LANES : (pair + 1) * 2 * LANES]
            product = dot(weight_ref[...], here, PLAIN)
            for i in range(2):
                d = pair * 2 + i
                other = arrived[d * PIECES // X][d % (X // PIECES)]
                total = block(product, i) + other.astype(F32)
                if d == 0:
                    keep_ref[...] = total
                    continue
                held_ref[d - 1] = total.astype(BF)
                copies.append(
                    pltpu.make_async_copy(held_ref.at[d - 1], sent[d - 1], sems.at[d - 1])
                )
                copies[-1].start()
        for copy in copies:
            copy.wait()

    part = shaped((depth, LANES), BF)
    outs = [shaped((depth, LANES), F32)] + [part] * (X - 1)
    scratch = staged(shaped((X - 1,) + part.shape, BF))
    flops = 2 * depth * width * X * LANES
    operands = [rows, weight, *arrived]
    keep, *sent = kernel_call(kernel, outs, flops, pos, operands, scratch, range(1, X))
    return keep, sent


def both_halves(pos, blocks, weight):
    depth, width = weight.shape
    count = 2 * X

    def kernel(pos_ref, *refs):
        weight_ref, out_ref, kept_ref, held_ref, out_sems, wide_ref, in_sems, sems = refs[-8:]
        x, c = pos_ref[0], pos_ref[1]
        arriving, leaving = [], []
        for index in range(count):
            part, d = divmod(index, X)
            here = wide_ref.at[part, :, pl.ds(d * LANES, LANES)]
            arriving.append(pltpu.make_async_copy(refs[index], here, in_sems.at[index]))
            arriving[-1].start()
        for part, half in ((0, c), (1, 1 - c)):
            for copy in arriving[part * X : (part + 1) * X]:
                copy.wait()
            kept = pltpu.make_async_copy(wide_ref.at[part], kept_ref.at[part], sems.at[part])
            kept.start()
            product = dot(weight_ref[...], wide_ref[part], PLAIN).astype(BF)
            for d in range(X):
                index, target = part * X + d, half * X + ((x + d) & 3)
                held_ref[index] = block(product, d)
                copy = pltpu.make_async_copy(
                    held_ref.at[index], out_ref.at[target], out_sems.at[index]
                )
                copy.start()
                leaving.append(copy)
            leaving.append(kept)
        for copy in leaving:
            copy.wait()

    outs = [shaped((count, depth, LANES), BF), shaped((2, width, X * LANES), BF)]
    flops = 2 * depth * width * count * LANES
    scratch = staged(outs[0]) + [pltpu.VMEM(outs[1].shape, BF)]
    scratch += [pltpu.SemaphoreType.DMA((count,)), pltpu.SemaphoreType.DMA((2,))]
    return kernel_call(
        kernel, outs, flops, pos, [*blocks, weight], scratch, (0, 1), range(count)
    )


def weight_grad(pos, factor, rows, blocks, rows_first):
    width, depth = rows.shape[1], blocks.shape[1]

    def kernel(pos_ref, rows_ref, blocks_ref, out_ref):
        x, c = pos_ref[0], pos_ref[1]
        total = None
        for part, half in ((0, c), (1, 1 - c)):
            pair = half_of(rows_ref, half, x), blocks_ref[part]
            term = dot(*(pair if rows_first else pair[::-1]), LAST)
            total = term if total is None else total + term
        out_ref[...] = (factor * total).astype(BF)

    outs = [shaped((width, depth) if rows_first else (depth, width), BF)]
    flops = 2 * depth * width * 2 * X * LANES
    return kernel_call(kernel, outs, flops, pos, [rows, blocks])[0]


def exchange(value, axis, groups=None):
    return lax.all_to_all(value, axis, 0, 0, axis_index_groups=groups)


def many(pos, value, count):
    def kernel(pos_ref, value_ref, out_ref, held_ref, sems):
        copy = pltpu.make_async_copy(value_ref, held_ref, sems.at[count])
        copy.start()
        copy.wait()
        copies = [
            pltpu.make_async_copy(held_ref, out_ref.at[index], sems.at[index])
            for index in range(count)
        ]
        for copy in copies:
            copy.start()
        for copy in copies:
            copy.wait()

    outs = [shaped((count,) + value.shape, BF)]
    scratch = [pltpu.VMEM(value.shape, BF), pltpu.SemaphoreType.DMA((count + 1,))]
    return kernel_call(kernel, outs, 0, pos, [value], scratch, (0,), (0,))[0]


def fan_out(value, held_ref, out_ref, sems):
    held_ref[...] = value
    copies = [
        pltpu.make_async_copy(held_ref, out_ref.at[index], sems.at[index]) for index in range(Z)
    ]
    for copy in copies:
        copy.start()
    return copies


def activated(pos, arrived):
    def kernel(pos_ref, arrived_ref, hidden_ref, out_ref, held_ref, sems):
        hidden = total_of(arrived_ref[...])
        cdf = 0.5 * (1.0 + lax.erf(hidden * (1.0 / math.sqrt(2.0))))
        copies = fan_out((hidden * cdf).astype(BF), held_ref, out_ref, sems)
        hidden_ref[...] = hidden
        for copy in copies:
            copy.wait()

    part = arrived.shape[1:]
    outs = [shaped(part, F32), shaped(arrived.shape, BF)]
    scratch = [pltpu.VMEM(part, BF), pltpu.SemaphoreType.DMA((Z,))]
    return kernel_call(kernel, outs, arrived.size, pos, [arrived], scratch, (1,))


def sloped(pos, arrived, hidden):
    def kernel(pos_ref, arrived_ref, hidden_ref, out_ref, held_ref, sems):
        deltas = total_of(arrived_ref[...]) * slope(hidden_ref[...])
        for copy in fan_out(deltas.astype(BF), held_ref, out_ref, sems):
            copy.wait()

    outs = [shaped(arrived.shape, BF)]
    scratch = [pltpu.VMEM(hidden.shape, BF), pltpu.SemaphoreType.DMA((Z,))]
    return kernel_call(kernel, outs, arrived.size, pos, [arrived, hidden], scratch, (0,))[0]


def added(pos, value):
    def kernel(pos_ref, value_ref, out_ref):
        total = value_ref[0].astype(F32)
        for index in range(1, value.shape[0]):
            total = total + value_ref[index].astype(F32)
        out_ref[...] = total.astype(BF)

    return kernel_call(kernel, [shaped(value.shape[1:], BF)], value.size, pos, [value])[0]


def swap_cores(value):
    return lax.ppermute(value, "rep", rep_pairs(0, 0, 1))


def move_x(value, d):
    return lax.ppermute(value, "rep", rep_pairs(d, 0, 0))


def total_of(value):
    return jnp.sum(value.astype(F32), axis=0)


def sum_x(keep, sent):
    arrived = lax.optimization_barrier(tuple(move_x(sent[d - 1], d) for d in range(1, X)))
    for part in arrived:
        keep = keep + part.astype(F32)
    return keep.astype(BF)


def scatter_z(value):
    value = value.reshape(Z, value.shape[0] // Z, LANES)
    return exchange(value, "rep", Z_GROUPS)


def spread_z(value):
    return exchange(value, "rep", Z_GROUPS).reshape(-1, LANES)


def spread_x(value):
    return [value] + [move_x(value, -d) for d in range(1, X)]


def with_other_half(own):
    return own + [swap_cores(part) for part in own]


def body(tokens, first_weight, second_weight, cotangent):
    factor = float(GRP * tokens.shape[0]) ** (-0.5)
    rep = lax.axis_index("rep")
    pos = jnp.stack([rep >> 3, rep & 1, (rep >> 1) & 3]).astype(jnp.int32)

    tok = exchange(many(pos, tokens.T, GRP), "grp")
    first_turned, second_turned, cots, tok = lax.optimization_barrier(
        (first_weight.T, second_weight.T, many(pos, cotangent.T, GRP), tok)
    )
    sent = other_half(pos, tok, first_turned)
    keep, sent = own_half(pos, tok, first_turned, [swap_cores(part) for part in sent])
    cot = exchange(after(cots, keep), "grp")
    value = sum_x(keep, sent)

    sent = other_half(pos, after(cot, keep), second_weight)
    keep, sent = own_half(pos, cot, second_weight, [swap_cores(part) for part in sent])

    hidden, active = activated(pos, after(scatter_z(value), keep))
    deltas = sloped(pos, scatter_z(sum_x(keep, sent)), hidden)

    act = with_other_half(spread_x(spread_z(active)))
    dlt = spread_x(spread_z(deltas))
    out, act = both_halves(pos, act, second_turned)
    out = exchange(out, "grp")
    second_grad = weight_grad(pos, factor, cot, act, False)
    dlt = with_other_half([dlt[0]] + [after(part, second_grad) for part in dlt[1:]])
    back, dlt = both_halves(pos, dlt, first_weight)
    back = exchange(back, "grp")
    first_grad = weight_grad(pos, factor, tok, dlt, True)
    return (added(pos, out).T, added(pos, back).T, first_grad, second_grad)


def solution(mesh):
    in_specs = (P("grp", "rep"), P("rep", "grp"), P("grp", "rep"), P("grp", "rep"))
    out_specs = (P("grp", "rep"), P("grp", "rep"), P("rep", "grp"), P("grp", "rep"))
    return jax.shard_map(body, mesh=mesh, in_specs=in_specs, out_specs=out_specs, check_vma=False)
```

```python
import math

import jax
import jax.numpy as jnp
from jax import lax
from jax.experimental import pallas as pl
from jax.experimental.pallas import tpu as pltpu
from jax.sharding import PartitionSpec as P

BF = jnp.bfloat16
F32 = jnp.float32
GRP = 8
X, Z, C = 4, 4, 2
LANES = 128
PIECES = 2


def rep_index(x, z, c):
    return (x * Z + z) * C + c


def rep_pairs(dx, dz, dc):
    return [
        (rep_index(x, z, c), rep_index((x + dx) % X, (z + dz) % Z, (c + dc) % C))
        for x in range(X)
        for z in range(Z)
        for c in range(C)
    ]


Z_GROUPS = [[rep_index(x, z, c) for z in range(Z)] for x in range(X) for c in range(C)]


def after(value, *others):
    return lax.optimization_barrier((value,) + others)[0]


def slope(hidden):
    normal_cdf = 0.5 * (1.0 + lax.erf(hidden * (1.0 / math.sqrt(2.0))))
    density = jnp.exp(-0.5 * hidden * hidden) * (1.0 / math.sqrt(2.0 * math.pi))
    return normal_cdf + hidden * density


def dot(left, right, dims):
    return lax.dot_general(left, right, (dims, ((), ())), preferred_element_type=F32)


PLAIN = ((1,), (0,))
LAST = ((1,), (1,))


def shaped(shape, dtype):
    return jax.ShapeDtypeStruct(shape, dtype)


def kernel_call(kernel, outs, flops, pos, operands, scratch=(), far=(), far_in=()):
    moved = sum(math.prod(o.shape) * o.dtype.itemsize for o in [*operands, *outs])
    vmem = pl.BlockSpec(memory_space=pltpu.VMEM)
    hbm = pl.BlockSpec(memory_space=pltpu.HBM)
    return pl.pallas_call(
        kernel,
        out_shape=[pltpu.HBM(o.shape, o.dtype) if i in far else o for i, o in enumerate(outs)],
        in_specs=[pl.BlockSpec(memory_space=pltpu.SMEM)]
        + [hbm if i in far_in else vmem for i in range(len(operands))],
        out_specs=[hbm if i in far else vmem for i in range(len(outs))],
        scratch_shapes=scratch,
        compiler_params=pltpu.CompilerParams(vmem_limit_bytes=16 * 1024 * 1024),
        cost_estimate=pl.CostEstimate(flops=flops, bytes_accessed=moved, transcendentals=0),
    )(pos, *operands)


def half_of(ref, half, x):
    return jnp.concatenate([ref[half * X + ((x + d) & 3)] for d in range(X)], axis=1)


def wide(refs):
    return jnp.concatenate([ref[...] for ref in refs], axis=1)


def block(value, d):
    return value[:, d * LANES : (d + 1) * LANES]


def staged(out):
    return [pltpu.VMEM(out.shape, out.dtype), pltpu.SemaphoreType.DMA(out.shape[:1])]


def other_half(pos, rows, weight):
    depth, width = weight.shape
    each = X // PIECES

    def kernel(pos_ref, rows_ref, weight_ref, *refs):
        outs, held_ref, sems = refs[:PIECES], refs[-2], refs[-1]
        rows = half_of(rows_ref, 1 - pos_ref[1], pos_ref[0])
        copies = []
        for pair in range(X // 2):
            here = rows[:, pair * 2 * LANES : (pair + 1) * 2 * LANES]
            product = dot(weight_ref[...], here, PLAIN).astype(BF)
            for d in range(2):
                index = pair * 2 + d
                held_ref[index] = block(product, d)
                target = outs[index // each].at[index % each]
                copies.append(pltpu.make_async_copy(held_ref.at[index], target, sems.at[index]))
                copies[-1].start()
        for copy in copies:
            copy.wait()

    outs = [shaped((each, depth, LANES), BF)] * PIECES
    flops = 2 * depth * width * X * LANES
    scratch = staged(shaped((X, depth, LANES), BF))
    return kernel_call(kernel, outs, flops, pos, [rows, weight], scratch, range(PIECES))


def own_half(pos, rows, weight, arrived):
    depth, width = weight.shape

    def kernel(pos_ref, rows_ref, weight_ref, *refs):
        arrived, keep_ref = refs[:PIECES], refs[PIECES]
        sent, held_ref, sems = refs[PIECES + 1 : -2], refs[-2], refs[-1]
        rows = half_of(rows_ref, pos_ref[1], pos_ref[0])
        copies = []
        for pair in (1, 0):
            here = rows[:, pair * 2 * LANES : (pair + 1) * 2 * LANES]
            product = dot(weight_ref[...], here, PLAIN)
            for i in range(2):
                d = pair * 2 + i
                other = arrived[d * PIECES // X][d % (X // PIECES)]
                total = block(product, i) + other.astype(F32)
                if d == 0:
                    keep_ref[...] = total
                    continue
                held_ref[d - 1] = total.astype(BF)
                copies.append(
                    pltpu.make_async_copy(held_ref.at[d - 1], sent[d - 1], sems.at[d - 1])
                )
                copies[-1].start()
        for copy in copies:
            copy.wait()

    part = shaped((depth, LANES), BF)
    outs = [shaped((depth, LANES), F32)] + [part] * (X - 1)
    scratch = staged(shaped((X - 1,) + part.shape, BF))
    flops = 2 * depth * width * X * LANES
    operands = [rows, weight, *arrived]
    keep, *sent = kernel_call(kernel, outs, flops, pos, operands, scratch, range(1, X))
    return keep, sent


def both_halves(pos, blocks, weight):
    depth, width = weight.shape
    count = 2 * X

    def kernel(pos_ref, *refs):
        weight_ref, out_ref, kept_ref, held_ref, out_sems, sems = refs[-6:]
        kept = [
            pltpu.make_async_copy(refs[index], kept_ref.at[index], sems.at[index])
            for index in range(count)
        ]
        for copy in kept:
            copy.start()
        x, c = pos_ref[0], pos_ref[1]
        for part, half in ((refs[:X], c), (refs[X:count], 1 - c)):
            product = dot(weight_ref[...], wide(part), PLAIN).astype(BF)
            for d in range(X):
                index, target = len(kept) - count, half * X + ((x + d) & 3)
                held_ref[index] = block(product, d)
                kept.append(
                    pltpu.make_async_copy(held_ref.at[index], out_ref.at[target], out_sems.at[index])
                )
                kept[-1].start()
        for copy in kept:
            copy.wait()

    outs = [shaped((count, depth, LANES), BF), shaped((count, width, LANES), BF)]
    flops = 2 * depth * width * count * LANES
    scratch = staged(outs[0]) + [pltpu.SemaphoreType.DMA((count,))]
    return kernel_call(kernel, outs, flops, pos, [*blocks, weight], scratch, (0, 1))


def weight_grad(pos, factor, rows, blocks, rows_first):
    width, depth = rows.shape[1], blocks.shape[1]

    def kernel(pos_ref, rows_ref, blocks_ref, out_ref):
        x, c = pos_ref[0], pos_ref[1]
        total = None
        for part, half in ((0, c), (1, 1 - c)):
            pair = half_of(rows_ref, half, x), half_of(blocks_ref, part, 0)
            term = dot(*(pair if rows_first else pair[::-1]), LAST)
            total = term if total is None else total + term
        out_ref[...] = (factor * total).astype(BF)

    outs = [shaped((width, depth) if rows_first else (depth, width), BF)]
    flops = 2 * depth * width * 2 * X * LANES
    return kernel_call(kernel, outs, flops, pos, [rows, blocks])[0]


def exchange(value, axis, groups=None):
    return lax.all_to_all(value, axis, 0, 0, axis_index_groups=groups)


def many(pos, value, count):
    def kernel(pos_ref, value_ref, out_ref, sems):
        copies = [
            pltpu.make_async_copy(value_ref, out_ref.at[index], sems.at[index])
            for index in range(count)
        ]
        for copy in copies:
            copy.start()
        for copy in copies:
            copy.wait()

    outs = [shaped((count,) + value.shape, BF)]
    scratch = [pltpu.SemaphoreType.DMA((count,))]
    return kernel_call(kernel, outs, 0, pos, [value], scratch, (0,))[0]


def fan_out(value, held_ref, out_ref, sems):
    held_ref[...] = value
    copies = [
        pltpu.make_async_copy(held_ref, out_ref.at[index], sems.at[index]) for index in range(Z)
    ]
    for copy in copies:
        copy.start()
    return copies


def activated(pos, arrived):
    def kernel(pos_ref, arrived_ref, hidden_ref, out_ref, held_ref, sems):
        hidden = total_of(arrived_ref[...])
        cdf = 0.5 * (1.0 + lax.erf(hidden * (1.0 / math.sqrt(2.0))))
        copies = fan_out((hidden * cdf).astype(BF), held_ref, out_ref, sems)
        hidden_ref[...] = hidden
        for copy in copies:
            copy.wait()

    part = arrived.shape[1:]
    outs = [shaped(part, F32), shaped(arrived.shape, BF)]
    scratch = [pltpu.VMEM(part, BF), pltpu.SemaphoreType.DMA((Z,))]
    return kernel_call(kernel, outs, arrived.size, pos, [arrived], scratch, (1,))


def sloped(pos, arrived, hidden):
    def kernel(pos_ref, arrived_ref, hidden_ref, out_ref, held_ref, sems):
        deltas = total_of(arrived_ref[...]) * slope(hidden_ref[...])
        for copy in fan_out(deltas.astype(BF), held_ref, out_ref, sems):
            copy.wait()

    outs = [shaped(arrived.shape, BF)]
    scratch = [pltpu.VMEM(hidden.shape, BF), pltpu.SemaphoreType.DMA((Z,))]
    return kernel_call(kernel, outs, arrived.size, pos, [arrived, hidden], scratch, (0,))[0]


def added(pos, value):
    def kernel(pos_ref, value_ref, out_ref):
        total = value_ref[0].astype(F32)
        for index in range(1, value.shape[0]):
            total = total + value_ref[index].astype(F32)
        out_ref[...] = total.astype(BF)

    return kernel_call(kernel, [shaped(value.shape[1:], BF)], value.size, pos, [value])[0]


def swap_cores(value):
    return lax.ppermute(value, "rep", rep_pairs(0, 0, 1))


def move_x(value, d):
    return lax.ppermute(value, "rep", rep_pairs(d, 0, 0))


def total_of(value):
    return jnp.sum(value.astype(F32), axis=0)


def sum_x(keep, sent):
    arrived = lax.optimization_barrier(tuple(move_x(sent[d - 1], d) for d in range(1, X)))
    for part in arrived:
        keep = keep + part.astype(F32)
    return keep.astype(BF)


def scatter_z(value):
    value = value.reshape(Z, value.shape[0] // Z, LANES)
    return exchange(value, "rep", Z_GROUPS)


def spread_z(value):
    return exchange(value, "rep", Z_GROUPS).reshape(-1, LANES)


def spread_x(value):
    return [value] + [move_x(value, -d) for d in range(1, X)]


def with_other_half(own):
    return own + [swap_cores(part) for part in own]


def body(tokens, first_weight, second_weight, cotangent):
    factor = float(GRP * tokens.shape[0]) ** (-0.5)
    rep = lax.axis_index("rep")
    pos = jnp.stack([rep >> 3, rep & 1, (rep >> 1) & 3]).astype(jnp.int32)

    tok = exchange(many(pos, tokens.T, GRP), "grp")
    first_turned, second_turned, cots, tok = lax.optimization_barrier(
        (first_weight.T, second_weight.T, many(pos, cotangent.T, GRP), tok)
    )
    sent = other_half(pos, tok, first_turned)
    keep, sent = own_half(pos, tok, first_turned, [swap_cores(part) for part in sent])
    cot = exchange(cots, "grp")
    value = sum_x(keep, sent)

    sent = other_half(pos, after(cot, keep), second_weight)
    keep, sent = own_half(pos, cot, second_weight, [swap_cores(part) for part in sent])

    hidden, active = activated(pos, after(scatter_z(value), keep))
    deltas = sloped(pos, scatter_z(sum_x(keep, sent)), hidden)

    act = with_other_half(spread_x(spread_z(active)))
    dlt = spread_x(spread_z(deltas))
    out, act = both_halves(pos, act, second_turned)
    out = exchange(out, "grp")
    second_grad = weight_grad(pos, factor, cot, act, False)
    dlt = with_other_half([dlt[0]] + [after(part, second_grad) for part in dlt[1:]])
    back, dlt = both_halves(pos, dlt, first_weight)
    back = exchange(back, "grp")
    first_grad = weight_grad(pos, factor, tok, dlt, True)
    return (added(pos, out).T, added(pos, back).T, first_grad, second_grad)


def solution(mesh):
    in_specs = (P("grp", "rep"), P("rep", "grp"), P("grp", "rep"), P("grp", "rep"))
    out_specs = (P("grp", "rep"), P("grp", "rep"), P("rep", "grp"), P("grp", "rep"))
    return jax.shard_map(body, mesh=mesh, in_specs=in_specs, out_specs=out_specs, check_vma=False)
```

```python
import math

import jax
import jax.numpy as jnp
from jax import lax
from jax.experimental import pallas as pl
from jax.experimental.pallas import tpu as pltpu
from jax.sharding import PartitionSpec as P

BF = jnp.bfloat16
F32 = jnp.float32
GRP = 8
X, Z, C = 4, 4, 2
LANES = 128
TILE = 16
PIECES = 2


def rep_index(x, z, c):
    return (x * Z + z) * C + c


def rep_pairs(dx, dz, dc):
    return [
        (rep_index(x, z, c), rep_index((x + dx) % X, (z + dz) % Z, (c + dc) % C))
        for x in range(X)
        for z in range(Z)
        for c in range(C)
    ]


Z_GROUPS = [[rep_index(x, z, c) for z in range(Z)] for x in range(X) for c in range(C)]


def after(value, *others):
    return lax.optimization_barrier((value,) + others)[0]


def slope(hidden):
    normal_cdf = 0.5 * (1.0 + lax.erf(hidden * (1.0 / math.sqrt(2.0))))
    density = jnp.exp(-0.5 * hidden * hidden) * (1.0 / math.sqrt(2.0 * math.pi))
    return normal_cdf + hidden * density


def dot(left, right, dims):
    return lax.dot_general(left, right, (dims, ((), ())), preferred_element_type=F32)


PLAIN = ((1,), (0,))
LAST = ((1,), (1,))


def shaped(shape, dtype):
    return jax.ShapeDtypeStruct(shape, dtype)


def kernel_call(kernel, outs, flops, pos, operands, scratch=(), far=(), far_in=()):
    moved = sum(math.prod(o.shape) * o.dtype.itemsize for o in [*operands, *outs])
    vmem = pl.BlockSpec(memory_space=pltpu.VMEM)
    hbm = pl.BlockSpec(memory_space=pltpu.HBM)
    return pl.pallas_call(
        kernel,
        out_shape=[pltpu.HBM(o.shape, o.dtype) if i in far else o for i, o in enumerate(outs)],
        in_specs=[pl.BlockSpec(memory_space=pltpu.SMEM)]
        + [hbm if i in far_in else vmem for i in range(len(operands))],
        out_specs=[hbm if i in far else vmem for i in range(len(outs))],
        scratch_shapes=scratch,
        compiler_params=pltpu.CompilerParams(vmem_limit_bytes=16 * 1024 * 1024),
        cost_estimate=pl.CostEstimate(flops=flops, bytes_accessed=moved, transcendentals=0),
    )(pos, *operands)


def half_of(ref, half, x):
    return jnp.concatenate([ref[half * X + ((x + d) & 3)] for d in range(X)], axis=1)


def wide(refs, rows):
    return jnp.concatenate([ref[:rows] for ref in refs], axis=1)


def block(value, d):
    return value[:, d * LANES : (d + 1) * LANES]


def staged(out):
    return [pltpu.VMEM(out.shape, out.dtype), pltpu.SemaphoreType.DMA(out.shape[:1])]


def other_half(pos, rows, weight):
    depth, width = weight.shape
    each = X // PIECES

    def kernel(pos_ref, rows_ref, weight_ref, *refs):
        outs, held_ref, sems = refs[:PIECES], refs[-2], refs[-1]
        rows = half_of(rows_ref, 1 - pos_ref[1], pos_ref[0])
        copies = []
        for pair in range(X // 2):
            here = rows[:, pair * 2 * LANES : (pair + 1) * 2 * LANES]
            product = dot(weight_ref[...], here, PLAIN).astype(BF)
            for d in range(2):
                index = pair * 2 + d
                held_ref[index] = block(product, d)
                target = outs[index // each].at[index % each]
                copies.append(pltpu.make_async_copy(held_ref.at[index], target, sems.at[index]))
                copies[-1].start()
        for copy in copies:
            copy.wait()

    outs = [shaped((each, depth, LANES), BF)] * PIECES
    flops = 2 * depth * width * X * LANES
    scratch = staged(shaped((X, depth, LANES), BF))
    return kernel_call(kernel, outs, flops, pos, [rows, weight], scratch, range(PIECES))


def own_half(pos, rows, weight, arrived):
    depth, width = weight.shape
    padded = -(-depth // (Z * TILE)) * Z * TILE

    def kernel(pos_ref, rows_ref, weight_ref, *refs):
        arrived, keep_ref = refs[:PIECES], refs[PIECES]
        sent, held_ref, sems = refs[PIECES + 1 : -2], refs[-2], refs[-1]
        rows = half_of(rows_ref, pos_ref[1], pos_ref[0])
        copies = []
        for pair in (1, 0):
            here = rows[:, pair * 2 * LANES : (pair + 1) * 2 * LANES]
            product = dot(weight_ref[...], here, PLAIN)
            for i in range(2):
                d = pair * 2 + i
                other = arrived[d * PIECES // X][d % (X // PIECES)]
                total = block(product, i) + other.astype(F32)
                if d == 0:
                    keep_ref[:depth] = total
                    keep_ref[depth:] = jnp.zeros((padded - depth, LANES), F32)
                    continue
                held_ref[d - 1, :depth] = total.astype(BF)
                held_ref[d - 1, depth:] = jnp.zeros((padded - depth, LANES), BF)
                copies.append(
                    pltpu.make_async_copy(held_ref.at[d - 1], sent[d - 1], sems.at[d - 1])
                )
                copies[-1].start()
        for copy in copies:
            copy.wait()

    part = shaped((padded, LANES), BF)
    outs = [shaped((padded, LANES), F32)] + [part] * (X - 1)
    scratch = staged(shaped((X - 1,) + part.shape, BF))
    flops = 2 * depth * width * X * LANES
    operands = [rows, weight, *arrived]
    keep, *sent = kernel_call(kernel, outs, flops, pos, operands, scratch, range(1, X))
    return keep, sent


def both_halves(pos, blocks, weight):
    depth, width = weight.shape
    count = 2 * X

    def kernel(pos_ref, *refs):
        weight_ref, out_ref, kept_ref, held_ref, out_sems, sems = refs[-6:]
        kept = [
            pltpu.make_async_copy(
                refs[index].at[pl.ds(0, width)], kept_ref.at[index], sems.at[index]
            )
            for index in range(count)
        ]
        for copy in kept:
            copy.start()
        x, c = pos_ref[0], pos_ref[1]
        for part, half in ((refs[:X], c), (refs[X:count], 1 - c)):
            product = dot(weight_ref[...], wide(part, width), PLAIN).astype(BF)
            for d in range(X):
                index, target = len(kept) - count, half * X + ((x + d) & 3)
                held_ref[index] = block(product, d)
                kept.append(
                    pltpu.make_async_copy(held_ref.at[index], out_ref.at[target], out_sems.at[index])
                )
                kept[-1].start()
        for copy in kept:
            copy.wait()

    outs = [shaped((count, depth, LANES), BF), shaped((count, width, LANES), BF)]
    flops = 2 * depth * width * count * LANES
    scratch = staged(outs[0]) + [pltpu.SemaphoreType.DMA((count,))]
    return kernel_call(kernel, outs, flops, pos, [*blocks, weight], scratch, (0, 1))


def weight_grad(pos, factor, rows, blocks, rows_first):
    width, depth = rows.shape[1], blocks.shape[1]

    def kernel(pos_ref, rows_ref, blocks_ref, out_ref):
        x, c = pos_ref[0], pos_ref[1]
        total = None
        for part, half in ((0, c), (1, 1 - c)):
            pair = half_of(rows_ref, half, x), half_of(blocks_ref, part, 0)
            term = dot(*(pair if rows_first else pair[::-1]), LAST)
            total = term if total is None else total + term
        out_ref[...] = (factor * total).astype(BF)

    outs = [shaped((width, depth) if rows_first else (depth, width), BF)]
    flops = 2 * depth * width * 2 * X * LANES
    return kernel_call(kernel, outs, flops, pos, [rows, blocks])[0]


def exchange(value, axis, groups=None):
    return lax.all_to_all(value, axis, 0, 0, axis_index_groups=groups)


def many(pos, value, count):
    def kernel(pos_ref, value_ref, out_ref, sems):
        copies = [
            pltpu.make_async_copy(value_ref, out_ref.at[index], sems.at[index])
            for index in range(count)
        ]
        for copy in copies:
            copy.start()
        for copy in copies:
            copy.wait()

    outs = [shaped((count,) + value.shape, BF)]
    scratch = [pltpu.SemaphoreType.DMA((count,))]
    return kernel_call(kernel, outs, 0, pos, [value], scratch, (0,))[0]


def fan_out(value, held_ref, out_ref, sems):
    held_ref[...] = value
    copies = [
        pltpu.make_async_copy(held_ref, out_ref.at[index], sems.at[index]) for index in range(Z)
    ]
    for copy in copies:
        copy.start()
    return copies


def activated(pos, arrived):
    def kernel(pos_ref, arrived_ref, hidden_ref, out_ref, held_ref, sems):
        hidden = total_of(arrived_ref[...])
        cdf = 0.5 * (1.0 + lax.erf(hidden * (1.0 / math.sqrt(2.0))))
        copies = fan_out((hidden * cdf).astype(BF), held_ref, out_ref, sems)
        hidden_ref[...] = hidden
        for copy in copies:
            copy.wait()

    part = arrived.shape[1:]
    outs = [shaped(part, F32), shaped(arrived.shape, BF)]
    scratch = [pltpu.VMEM(part, BF), pltpu.SemaphoreType.DMA((Z,))]
    return kernel_call(kernel, outs, arrived.size, pos, [arrived], scratch, (1,))


def sloped(pos, arrived, hidden):
    def kernel(pos_ref, arrived_ref, hidden_ref, out_ref, held_ref, sems):
        deltas = total_of(arrived_ref[...]) * slope(hidden_ref[...])
        for copy in fan_out(deltas.astype(BF), held_ref, out_ref, sems):
            copy.wait()

    outs = [shaped(arrived.shape, BF)]
    scratch = [pltpu.VMEM(hidden.shape, BF), pltpu.SemaphoreType.DMA((Z,))]
    return kernel_call(kernel, outs, arrived.size, pos, [arrived, hidden], scratch, (0,))[0]


def added(pos, value):
    def kernel(pos_ref, value_ref, out_ref):
        total = value_ref[0].astype(F32)
        for index in range(1, value.shape[0]):
            total = total + value_ref[index].astype(F32)
        out_ref[...] = total.astype(BF)

    return kernel_call(kernel, [shaped(value.shape[1:], BF)], value.size, pos, [value])[0]


def swap_cores(value):
    return lax.ppermute(value, "rep", rep_pairs(0, 0, 1))


def move_x(value, d):
    return lax.ppermute(value, "rep", rep_pairs(d, 0, 0))


def total_of(value):
    return jnp.sum(value.astype(F32), axis=0)


def sum_x(keep, sent):
    arrived = lax.optimization_barrier(tuple(move_x(sent[d - 1], d) for d in range(1, X)))
    for part in arrived:
        keep = keep + part.astype(F32)
    return keep.astype(BF)


def scatter_z(value):
    return exchange(value.reshape(Z, value.shape[0] // Z, LANES), "rep", Z_GROUPS)


def spread_z(value):
    return exchange(value, "rep", Z_GROUPS).reshape(-1, LANES)


def spread_x(value):
    return [value] + [move_x(value, -d) for d in range(1, X)]


def with_other_half(own):
    return own + [swap_cores(part) for part in own]


def body(tokens, first_weight, second_weight, cotangent):
    factor = float(GRP * tokens.shape[0]) ** (-0.5)
    rep = lax.axis_index("rep")
    pos = jnp.stack([rep >> 3, rep & 1, (rep >> 1) & 3]).astype(jnp.int32)

    tok = exchange(many(pos, tokens.T, GRP), "grp")
    first_turned, second_turned, cots, tok = lax.optimization_barrier(
        (first_weight.T, second_weight.T, many(pos, cotangent.T, GRP), tok)
    )
    sent = other_half(pos, tok, first_turned)
    keep, sent = own_half(pos, tok, first_turned, [swap_cores(part) for part in sent])
    cot = exchange(after(cots, keep), "grp")
    value = sum_x(keep, sent)

    sent = other_half(pos, after(cot, keep), second_weight)
    keep, sent = own_half(pos, cot, second_weight, [swap_cores(part) for part in sent])

    hidden, active = activated(pos, after(scatter_z(value), keep))
    deltas = sloped(pos, scatter_z(sum_x(keep, sent)), hidden)

    act = with_other_half(spread_x(spread_z(active)))
    dlt = spread_x(spread_z(deltas))
    out, act = both_halves(pos, act, second_turned)
    out = exchange(out, "grp")
    second_grad = weight_grad(pos, factor, cot, act, False)
    dlt = with_other_half([dlt[0]] + [after(part, second_grad) for part in dlt[1:]])
    back, dlt = both_halves(pos, dlt, first_weight)
    back = exchange(back, "grp")
    first_grad = weight_grad(pos, factor, tok, dlt, True)
    return (added(pos, out).T, added(pos, back).T, first_grad, second_grad)


def solution(mesh):
    in_specs = (P("grp", "rep"), P("rep", "grp"), P("grp", "rep"), P("grp", "rep"))
    out_specs = (P("grp", "rep"), P("grp", "rep"), P("rep", "grp"), P("grp", "rep"))
    return jax.shard_map(body, mesh=mesh, in_specs=in_specs, out_specs=out_specs, check_vma=False)
```

```python
import math

import jax
import jax.numpy as jnp
from jax import lax
from jax.experimental import pallas as pl
from jax.experimental.pallas import tpu as pltpu
from jax.sharding import PartitionSpec as P

BF = jnp.bfloat16
F32 = jnp.float32
GRP = 8
X, Z, C = 4, 4, 2
LANES = 128
TILE = 16
PIECES = 2


def rep_index(x, z, c):
    return (x * Z + z) * C + c


def rep_pairs(dx, dz, dc):
    return [
        (rep_index(x, z, c), rep_index((x + dx) % X, (z + dz) % Z, (c + dc) % C))
        for x in range(X)
        for z in range(Z)
        for c in range(C)
    ]


Z_GROUPS = [[rep_index(x, z, c) for z in range(Z)] for x in range(X) for c in range(C)]


def after(value, *others):
    return lax.optimization_barrier((value,) + others)[0]


def slope(hidden):
    normal_cdf = 0.5 * (1.0 + lax.erf(hidden * (1.0 / math.sqrt(2.0))))
    density = jnp.exp(-0.5 * hidden * hidden) * (1.0 / math.sqrt(2.0 * math.pi))
    return normal_cdf + hidden * density


def dot(left, right, dims):
    return lax.dot_general(left, right, (dims, ((), ())), preferred_element_type=F32)


PLAIN = ((1,), (0,))
LAST = ((1,), (1,))


def shaped(shape, dtype):
    return jax.ShapeDtypeStruct(shape, dtype)


def kernel_call(kernel, outs, flops, pos, operands, scratch=(), far=(), far_in=()):
    moved = sum(math.prod(o.shape) * o.dtype.itemsize for o in [*operands, *outs])
    vmem = pl.BlockSpec(memory_space=pltpu.VMEM)
    hbm = pl.BlockSpec(memory_space=pltpu.HBM)
    anywhere = pl.BlockSpec(memory_space=pl.ANY)
    return pl.pallas_call(
        kernel,
        out_shape=[pltpu.HBM(o.shape, o.dtype) if i in far else o for i, o in enumerate(outs)],
        in_specs=[pl.BlockSpec(memory_space=pltpu.SMEM)]
        + [anywhere if i in far_in else vmem for i in range(len(operands))],
        out_specs=[hbm if i in far else vmem for i in range(len(outs))],
        scratch_shapes=scratch,
        compiler_params=pltpu.CompilerParams(vmem_limit_bytes=16 * 1024 * 1024),
        cost_estimate=pl.CostEstimate(flops=flops, bytes_accessed=moved, transcendentals=0),
    )(pos, *operands)


def half_of(ref, half, x):
    return jnp.concatenate([ref[half * X + ((x + d) & 3)] for d in range(X)], axis=1)


def wide(refs, rows):
    return jnp.concatenate([ref[:rows] for ref in refs], axis=1)


def block(value, d):
    return value[:, d * LANES : (d + 1) * LANES]


def staged(out):
    return [pltpu.VMEM(out.shape, out.dtype), pltpu.SemaphoreType.DMA(out.shape[:1])]


def other_half(pos, rows, weight):
    depth, width = weight.shape
    each = X // PIECES

    def kernel(pos_ref, rows_ref, weight_ref, *refs):
        outs, held_ref, sems = refs[:PIECES], refs[-2], refs[-1]
        rows = half_of(rows_ref, 1 - pos_ref[1], pos_ref[0])
        copies = []
        for pair in range(X // 2):
            here = rows[:, pair * 2 * LANES : (pair + 1) * 2 * LANES]
            product = dot(weight_ref[...], here, PLAIN).astype(BF)
            for d in range(2):
                index = pair * 2 + d
                held_ref[index] = block(product, d)
                target = outs[index // each].at[index % each]
                copies.append(pltpu.make_async_copy(held_ref.at[index], target, sems.at[index]))
                copies[-1].start()
        for copy in copies:
            copy.wait()

    outs = [shaped((each, depth, LANES), BF)] * PIECES
    flops = 2 * depth * width * X * LANES
    scratch = staged(shaped((X, depth, LANES), BF))
    return kernel_call(kernel, outs, flops, pos, [rows, weight], scratch, range(PIECES))


def own_half(pos, rows, weight, arrived):
    depth, width = weight.shape
    padded = -(-depth // (Z * TILE)) * Z * TILE

    def kernel(pos_ref, rows_ref, weight_ref, *refs):
        arrived, keep_ref = refs[:PIECES], refs[PIECES]
        sent, (held_ref, sems, near_ref, near_sems) = refs[PIECES + 1 : -4], refs[-4:]
        arriving = [
            pltpu.make_async_copy(arrived[p], near_ref.at[p], near_sems.at[p])
            for p in range(PIECES)
        ]
        for copy in arriving[::-1]:
            copy.start()
        rows = half_of(rows_ref, pos_ref[1], pos_ref[0])
        copies = []
        for pair in (1, 0):
            here = rows[:, pair * 2 * LANES : (pair + 1) * 2 * LANES]
            product = dot(weight_ref[...], here, PLAIN)
            arriving[pair].wait()
            for i in range(2):
                d = pair * 2 + i
                other = near_ref[pair, i]
                total = block(product, i) + other.astype(F32)
                if d == 0:
                    keep_ref[:depth] = total
                    keep_ref[depth:] = jnp.zeros((padded - depth, LANES), F32)
                    continue
                held_ref[d - 1, :depth] = total.astype(BF)
                held_ref[d - 1, depth:] = jnp.zeros((padded - depth, LANES), BF)
                copies.append(
                    pltpu.make_async_copy(held_ref.at[d - 1], sent[d - 1], sems.at[d - 1])
                )
                copies[-1].start()
        for copy in copies:
            copy.wait()

    part = shaped((padded, LANES), BF)
    outs = [shaped((padded, LANES), F32)] + [part] * (X - 1)
    scratch = staged(shaped((X - 1,) + part.shape, BF))
    scratch += staged(shaped((PIECES,) + arrived[0].shape, BF))
    flops = 2 * depth * width * X * LANES
    operands = [rows, weight, *arrived]
    keep, *sent = kernel_call(
        kernel, outs, flops, pos, operands, scratch, range(1, X), range(2, 2 + PIECES)
    )
    return keep, sent


def both_halves(pos, blocks, weight):
    depth, width = weight.shape
    count = 2 * X

    def kernel(pos_ref, *refs):
        weight_ref, out_ref, kept_ref, held_ref, out_sems, sems = refs[-6:]
        kept = [
            pltpu.make_async_copy(
                refs[index].at[pl.ds(0, width)], kept_ref.at[index], sems.at[index]
            )
            for index in range(count)
        ]
        for copy in kept:
            copy.start()
        x, c = pos_ref[0], pos_ref[1]
        for part, half in ((refs[:X], c), (refs[X:count], 1 - c)):
            product = dot(weight_ref[...], wide(part, width), PLAIN).astype(BF)
            for d in range(X):
                index, target = len(kept) - count, half * X + ((x + d) & 3)
                held_ref[index] = block(product, d)
                kept.append(
                    pltpu.make_async_copy(held_ref.at[index], out_ref.at[target], out_sems.at[index])
                )
                kept[-1].start()
        for copy in kept:
            copy.wait()

    outs = [shaped((count, depth, LANES), BF), shaped((count, width, LANES), BF)]
    flops = 2 * depth * width * count * LANES
    scratch = staged(outs[0]) + [pltpu.SemaphoreType.DMA((count,))]
    return kernel_call(kernel, outs, flops, pos, [*blocks, weight], scratch, (0, 1))


def weight_grad(pos, factor, rows, blocks, rows_first):
    width, depth = rows.shape[1], blocks.shape[1]

    def kernel(pos_ref, rows_ref, blocks_ref, out_ref):
        x, c = pos_ref[0], pos_ref[1]
        total = None
        for part, half in ((0, c), (1, 1 - c)):
            pair = half_of(rows_ref, half, x), half_of(blocks_ref, part, 0)
            term = dot(*(pair if rows_first else pair[::-1]), LAST)
            total = term if total is None else total + term
        out_ref[...] = (factor * total).astype(BF)

    outs = [shaped((width, depth) if rows_first else (depth, width), BF)]
    flops = 2 * depth * width * 2 * X * LANES
    return kernel_call(kernel, outs, flops, pos, [rows, blocks])[0]


def exchange(value, axis, groups=None):
    return lax.all_to_all(value, axis, 0, 0, axis_index_groups=groups)


def many(pos, value, count):
    def kernel(pos_ref, value_ref, out_ref, sems):
        copies = [
            pltpu.make_async_copy(value_ref, out_ref.at[index], sems.at[index])
            for index in range(count)
        ]
        for copy in copies:
            copy.start()
        for copy in copies:
            copy.wait()

    outs = [shaped((count,) + value.shape, BF)]
    scratch = [pltpu.SemaphoreType.DMA((count,))]
    return kernel_call(kernel, outs, 0, pos, [value], scratch, (0,))[0]


def fan_out(value, held_ref, out_ref, sems):
    held_ref[...] = value
    copies = [
        pltpu.make_async_copy(held_ref, out_ref.at[index], sems.at[index]) for index in range(Z)
    ]
    for copy in copies:
        copy.start()
    return copies


def activated(pos, arrived):
    def kernel(pos_ref, arrived_ref, hidden_ref, out_ref, held_ref, sems):
        hidden = total_of(arrived_ref[...])
        cdf = 0.5 * (1.0 + lax.erf(hidden * (1.0 / math.sqrt(2.0))))
        copies = fan_out((hidden * cdf).astype(BF), held_ref, out_ref, sems)
        hidden_ref[...] = hidden
        for copy in copies:
            copy.wait()

    part = arrived.shape[1:]
    outs = [shaped(part, F32), shaped(arrived.shape, BF)]
    scratch = [pltpu.VMEM(part, BF), pltpu.SemaphoreType.DMA((Z,))]
    return kernel_call(kernel, outs, arrived.size, pos, [arrived], scratch, (1,))


def sloped(pos, arrived, hidden):
    def kernel(pos_ref, arrived_ref, hidden_ref, out_ref, held_ref, sems):
        deltas = total_of(arrived_ref[...]) * slope(hidden_ref[...])
        for copy in fan_out(deltas.astype(BF), held_ref, out_ref, sems):
            copy.wait()

    outs = [shaped(arrived.shape, BF)]
    scratch = [pltpu.VMEM(hidden.shape, BF), pltpu.SemaphoreType.DMA((Z,))]
    return kernel_call(kernel, outs, arrived.size, pos, [arrived, hidden], scratch, (0,))[0]


def added(pos, value):
    def kernel(pos_ref, value_ref, out_ref):
        total = value_ref[0].astype(F32)
        for index in range(1, value.shape[0]):
            total = total + value_ref[index].astype(F32)
        out_ref[...] = total.astype(BF)

    return kernel_call(kernel, [shaped(value.shape[1:], BF)], value.size, pos, [value])[0]


def swap_cores(value):
    return lax.ppermute(value, "rep", rep_pairs(0, 0, 1))


def move_x(value, d):
    return lax.ppermute(value, "rep", rep_pairs(d, 0, 0))


def total_of(value):
    return jnp.sum(value.astype(F32), axis=0)


def sum_x(keep, sent):
    arrived = lax.optimization_barrier(tuple(move_x(sent[d - 1], d) for d in range(1, X)))
    for part in arrived:
        keep = keep + part.astype(F32)
    return keep.astype(BF)


def scatter_z(value):
    return exchange(value.reshape(Z, value.shape[0] // Z, LANES), "rep", Z_GROUPS)


def spread_z(value):
    return exchange(value, "rep", Z_GROUPS).reshape(-1, LANES)


def spread_x(value):
    return [value] + [move_x(value, -d) for d in range(1, X)]


def with_other_half(own):
    return own + [swap_cores(part) for part in own]


def body(tokens, first_weight, second_weight, cotangent):
    factor = float(GRP * tokens.shape[0]) ** (-0.5)
    rep = lax.axis_index("rep")
    pos = jnp.stack([rep >> 3, rep & 1, (rep >> 1) & 3]).astype(jnp.int32)

    tok = exchange(many(pos, tokens.T, GRP), "grp")
    first_turned, second_turned, cots, tok = lax.optimization_barrier(
        (first_weight.T, second_weight.T, many(pos, cotangent.T, GRP), tok)
    )
    sent = other_half(pos, tok, first_turned)
    keep, sent = own_half(pos, tok, first_turned, [swap_cores(part) for part in sent])
    cot = exchange(after(cots, keep), "grp")
    value = sum_x(keep, sent)

    sent = other_half(pos, after(cot, keep), second_weight)
    keep, sent = own_half(pos, cot, second_weight, [swap_cores(part) for part in sent])

    hidden, active = activated(pos, after(scatter_z(value), keep))
    deltas = sloped(pos, scatter_z(sum_x(keep, sent)), hidden)

    act = with_other_half(spread_x(spread_z(active)))
    dlt = spread_x(spread_z(deltas))
    out, act = both_halves(pos, act, second_turned)
    out = exchange(out, "grp")
    second_grad = weight_grad(pos, factor, cot, act, False)
    dlt = with_other_half([dlt[0]] + [after(part, second_grad) for part in dlt[1:]])
    back, dlt = both_halves(pos, dlt, first_weight)
    back = exchange(back, "grp")
    first_grad = weight_grad(pos, factor, tok, dlt, True)
    return (added(pos, out).T, added(pos, back).T, first_grad, second_grad)


def solution(mesh):
    in_specs = (P("grp", "rep"), P("rep", "grp"), P("grp", "rep"), P("grp", "rep"))
    out_specs = (P("grp", "rep"), P("grp", "rep"), P("rep", "grp"), P("grp", "rep"))
    return jax.shard_map(body, mesh=mesh, in_specs=in_specs, out_specs=out_specs, check_vma=False)
```

```python
import math

import jax
import jax.numpy as jnp
from jax import lax
from jax.experimental import pallas as pl
from jax.experimental.pallas import tpu as pltpu
from jax.sharding import PartitionSpec as P

BF = jnp.bfloat16
F32 = jnp.float32
GRP = 8
X, Z, C = 4, 4, 2
LANES = 128
TILE = 16
PIECES = 2


def rep_index(x, z, c):
    return (x * Z + z) * C + c


def rep_pairs(dx, dz, dc):
    return [
        (rep_index(x, z, c), rep_index((x + dx) % X, (z + dz) % Z, (c + dc) % C))
        for x in range(X)
        for z in range(Z)
        for c in range(C)
    ]


Z_GROUPS = [[rep_index(x, z, c) for z in range(Z)] for x in range(X) for c in range(C)]


def after(value, *others):
    return lax.optimization_barrier((value,) + others)[0]


def slope(hidden):
    normal_cdf = 0.5 * (1.0 + lax.erf(hidden * (1.0 / math.sqrt(2.0))))
    density = jnp.exp(-0.5 * hidden * hidden) * (1.0 / math.sqrt(2.0 * math.pi))
    return normal_cdf + hidden * density


def dot(left, right, dims):
    return lax.dot_general(left, right, (dims, ((), ())), preferred_element_type=F32)


PLAIN = ((1,), (0,))
LAST = ((1,), (1,))


def shaped(shape, dtype):
    return jax.ShapeDtypeStruct(shape, dtype)


def kernel_call(kernel, outs, flops, pos, operands, scratch=(), far=(), far_in=()):
    moved = sum(math.prod(o.shape) * o.dtype.itemsize for o in [*operands, *outs])
    vmem = pl.BlockSpec(memory_space=pltpu.VMEM)
    hbm = pl.BlockSpec(memory_space=pltpu.HBM)
    return pl.pallas_call(
        kernel,
        out_shape=[pltpu.HBM(o.shape, o.dtype) if i in far else o for i, o in enumerate(outs)],
        in_specs=[pl.BlockSpec(memory_space=pltpu.SMEM)]
        + [hbm if i in far_in else vmem for i in range(len(operands))],
        out_specs=[hbm if i in far else vmem for i in range(len(outs))],
        scratch_shapes=scratch,
        compiler_params=pltpu.CompilerParams(vmem_limit_bytes=16 * 1024 * 1024),
        cost_estimate=pl.CostEstimate(flops=flops, bytes_accessed=moved, transcendentals=0),
    )(pos, *operands)


def half_of(ref, half, x):
    return jnp.concatenate([ref[half * X + ((x + d) & 3)] for d in range(X)], axis=1)


def wide(refs, rows):
    return jnp.concatenate([ref[:rows] for ref in refs], axis=1)


def block(value, d):
    return value[:, d * LANES : (d + 1) * LANES]


def staged(out):
    return [pltpu.VMEM(out.shape, out.dtype), pltpu.SemaphoreType.DMA(out.shape[:1])]


def other_half(pos, rows, weight):
    depth, width = weight.shape
    each = X // PIECES

    def kernel(pos_ref, rows_ref, weight_ref, *refs):
        outs, held_ref, sems = refs[:PIECES], refs[-2], refs[-1]
        rows = half_of(rows_ref, 1 - pos_ref[1], pos_ref[0])
        copies = []
        product = dot(weight_ref[...], rows, PLAIN).astype(BF)
        for pair in range(X // 2):
            for d in range(2):
                index = pair * 2 + d
                held_ref[index] = block(product, index)
                target = outs[index // each].at[index % each]
                copies.append(pltpu.make_async_copy(held_ref.at[index], target, sems.at[index]))
                copies[-1].start()
        for copy in copies:
            copy.wait()

    outs = [shaped((each, depth, LANES), BF)] * PIECES
    flops = 2 * depth * width * X * LANES
    scratch = staged(shaped((X, depth, LANES), BF))
    return kernel_call(kernel, outs, flops, pos, [rows, weight], scratch, range(PIECES))


def own_half(pos, rows, weight, arrived):
    depth, width = weight.shape
    padded = -(-depth // (Z * TILE)) * Z * TILE

    def kernel(pos_ref, rows_ref, weight_ref, *refs):
        arrived, keep_ref = refs[:PIECES], refs[PIECES]
        sent, held_ref, sems = refs[PIECES + 1 : -2], refs[-2], refs[-1]
        rows = half_of(rows_ref, pos_ref[1], pos_ref[0])
        copies = []
        for pair in (1, 0):
            here = rows[:, pair * 2 * LANES : (pair + 1) * 2 * LANES]
            product = dot(weight_ref[...], here, PLAIN)
            for i in range(2):
                d = pair * 2 + i
                other = arrived[d * PIECES // X][d % (X // PIECES)]
                total = block(product, i) + other.astype(F32)
                if d == 0:
                    keep_ref[:depth] = total
                    keep_ref[depth:] = jnp.zeros((padded - depth, LANES), F32)
                    continue
                held_ref[d - 1, :depth] = total.astype(BF)
                held_ref[d - 1, depth:] = jnp.zeros((padded - depth, LANES), BF)
                copies.append(
                    pltpu.make_async_copy(held_ref.at[d - 1], sent[d - 1], sems.at[d - 1])
                )
                copies[-1].start()
        for copy in copies:
            copy.wait()

    part = shaped((padded, LANES), BF)
    outs = [shaped((padded, LANES), F32)] + [part] * (X - 1)
    scratch = staged(shaped((X - 1,) + part.shape, BF))
    flops = 2 * depth * width * X * LANES
    operands = [rows, weight, *arrived]
    keep, *sent = kernel_call(kernel, outs, flops, pos, operands, scratch, range(1, X))
    return keep, sent


def both_halves(pos, blocks, weight):
    depth, width = weight.shape
    count = 2 * X

    def kernel(pos_ref, *refs):
        weight_ref, out_ref, kept_ref, held_ref, out_sems, sems = refs[-6:]
        kept = [
            pltpu.make_async_copy(
                refs[index].at[pl.ds(0, width)], kept_ref.at[index], sems.at[index]
            )
            for index in range(count)
        ]
        for copy in kept:
            copy.start()
        x, c = pos_ref[0], pos_ref[1]
        for part, half in ((refs[:X], c), (refs[X:count], 1 - c)):
            product = dot(weight_ref[...], wide(part, width), PLAIN).astype(BF)
            for d in range(X):
                index, target = len(kept) - count, half * X + ((x + d) & 3)
                held_ref[index] = block(product, d)
                kept.append(
                    pltpu.make_async_copy(held_ref.at[index], out_ref.at[target], out_sems.at[index])
                )
                kept[-1].start()
        for copy in kept:
            copy.wait()

    outs = [shaped((count, depth, LANES), BF), shaped((count, width, LANES), BF)]
    flops = 2 * depth * width * count * LANES
    scratch = staged(outs[0]) + [pltpu.SemaphoreType.DMA((count,))]
    return kernel_call(kernel, outs, flops, pos, [*blocks, weight], scratch, (0, 1))


def weight_grad(pos, factor, rows, blocks, rows_first):
    width, depth = rows.shape[1], blocks.shape[1]

    def kernel(pos_ref, rows_ref, blocks_ref, out_ref):
        x, c = pos_ref[0], pos_ref[1]
        total = None
        for part, half in ((0, c), (1, 1 - c)):
            pair = half_of(rows_ref, half, x), half_of(blocks_ref, part, 0)
            term = dot(*(pair if rows_first else pair[::-1]), LAST)
            total = term if total is None else total + term
        out_ref[...] = (factor * total).astype(BF)

    outs = [shaped((width, depth) if rows_first else (depth, width), BF)]
    flops = 2 * depth * width * 2 * X * LANES
    return kernel_call(kernel, outs, flops, pos, [rows, blocks])[0]


def exchange(value, axis, groups=None):
    return lax.all_to_all(value, axis, 0, 0, axis_index_groups=groups)


def many(pos, value, count):
    def kernel(pos_ref, value_ref, out_ref, sems):
        copies = [
            pltpu.make_async_copy(value_ref, out_ref.at[index], sems.at[index])
            for index in range(count)
        ]
        for copy in copies:
            copy.start()
        for copy in copies:
            copy.wait()

    outs = [shaped((count,) + value.shape, BF)]
    scratch = [pltpu.SemaphoreType.DMA((count,))]
    return kernel_call(kernel, outs, 0, pos, [value], scratch, (0,))[0]


def fan_out(value, held_ref, out_ref, sems):
    held_ref[...] = value
    copies = [
        pltpu.make_async_copy(held_ref, out_ref.at[index], sems.at[index]) for index in range(Z)
    ]
    for copy in copies:
        copy.start()
    return copies


def activated(pos, arrived):
    def kernel(pos_ref, arrived_ref, hidden_ref, out_ref, held_ref, sems):
        hidden = total_of(arrived_ref[...])
        cdf = 0.5 * (1.0 + lax.erf(hidden * (1.0 / math.sqrt(2.0))))
        copies = fan_out((hidden * cdf).astype(BF), held_ref, out_ref, sems)
        hidden_ref[...] = hidden
        for copy in copies:
            copy.wait()

    part = arrived.shape[1:]
    outs = [shaped(part, F32), shaped(arrived.shape, BF)]
    scratch = [pltpu.VMEM(part, BF), pltpu.SemaphoreType.DMA((Z,))]
    return kernel_call(kernel, outs, arrived.size, pos, [arrived], scratch, (1,))


def sloped(pos, arrived, hidden):
    def kernel(pos_ref, arrived_ref, hidden_ref, out_ref, held_ref, sems):
        deltas = total_of(arrived_ref[...]) * slope(hidden_ref[...])
        for copy in fan_out(deltas.astype(BF), held_ref, out_ref, sems):
            copy.wait()

    outs = [shaped(arrived.shape, BF)]
    scratch = [pltpu.VMEM(hidden.shape, BF), pltpu.SemaphoreType.DMA((Z,))]
    return kernel_call(kernel, outs, arrived.size, pos, [arrived, hidden], scratch, (0,))[0]


def added(pos, value):
    def kernel(pos_ref, value_ref, out_ref):
        total = value_ref[0].astype(F32)
        for index in range(1, value.shape[0]):
            total = total + value_ref[index].astype(F32)
        out_ref[...] = total.astype(BF)

    return kernel_call(kernel, [shaped(value.shape[1:], BF)], value.size, pos, [value])[0]


def swap_cores(value):
    return lax.ppermute(value, "rep", rep_pairs(0, 0, 1))


def move_x(value, d):
    return lax.ppermute(value, "rep", rep_pairs(d, 0, 0))


def total_of(value):
    return jnp.sum(value.astype(F32), axis=0)


def sum_x(keep, sent):
    arrived = lax.optimization_barrier(tuple(move_x(sent[d - 1], d) for d in range(1, X)))
    for part in arrived:
        keep = keep + part.astype(F32)
    return keep.astype(BF)


def scatter_z(value):
    return exchange(value.reshape(Z, value.shape[0] // Z, LANES), "rep", Z_GROUPS)


def spread_z(value):
    return exchange(value, "rep", Z_GROUPS).reshape(-1, LANES)


def spread_x(value):
    return [value] + [move_x(value, -d) for d in range(1, X)]


def with_other_half(own):
    return own + [swap_cores(part) for part in own]


def body(tokens, first_weight, second_weight, cotangent):
    factor = float(GRP * tokens.shape[0]) ** (-0.5)
    rep = lax.axis_index("rep")
    pos = jnp.stack([rep >> 3, rep & 1, (rep >> 1) & 3]).astype(jnp.int32)

    tok = exchange(many(pos, tokens.T, GRP), "grp")
    first_turned, second_turned, cots, tok = lax.optimization_barrier(
        (first_weight.T, second_weight.T, many(pos, cotangent.T, GRP), tok)
    )
    sent = other_half(pos, tok, first_turned)
    keep, sent = own_half(pos, tok, first_turned, [swap_cores(part) for part in sent])
    cot = exchange(after(cots, keep), "grp")
    value = sum_x(keep, sent)

    sent = other_half(pos, after(cot, keep), second_weight)
    keep, sent = own_half(pos, cot, second_weight, [swap_cores(part) for part in sent])

    hidden, active = activated(pos, after(scatter_z(value), keep))
    deltas = sloped(pos, scatter_z(sum_x(keep, sent)), hidden)

    act = with_other_half(spread_x(spread_z(active)))
    dlt = spread_x(spread_z(deltas))
    out, act = both_halves(pos, act, second_turned)
    out = exchange(out, "grp")
    second_grad = weight_grad(pos, factor, cot, act, False)
    dlt = with_other_half([dlt[0]] + [after(part, second_grad) for part in dlt[1:]])
    back, dlt = both_halves(pos, dlt, first_weight)
    back = exchange(back, "grp")
    first_grad = weight_grad(pos, factor, tok, dlt, True)
    return (added(pos, out).T, added(pos, back).T, first_grad, second_grad)


def solution(mesh):
    in_specs = (P("grp", "rep"), P("rep", "grp"), P("grp", "rep"), P("grp", "rep"))
    out_specs = (P("grp", "rep"), P("grp", "rep"), P("rep", "grp"), P("grp", "rep"))
    return jax.shard_map(body, mesh=mesh, in_specs=in_specs, out_specs=out_specs, check_vma=False)
```
